256 devices in a mesh: dom: 64 (over x, z, core), feat: 4 (over y).
Axes of the slice: x: 4, y: 4, z: 8, core: 2. Of those that a mesh axis runs over, the one named last changes fastest.
Arguments:
- node_feats: bfloat16 [128, 851968], P('feat', 'dom'), may hold values from -6 to 6
- adj_cols: int32 [6656, 2], P('dom'), may hold values from 0 to 231, as said below
- adj_vals: bfloat16 [6656, 2, 128, 128], P('dom'), may hold values from -0.375 to 0.375
- send_list: int32 [4096, 2], replicated, may hold values from 0 to 3, as said below
- send_count: int32 [4096], replicated, may hold values from 0 to 2, as said below
- w_self: bfloat16 [128, 256], replicated, may hold values from -0.5 to 0.5
- w_neigh: bfloat16 [128, 256], replicated, may hold values from -0.5 to 0.5
- cotangent: bfloat16 [851968, 256], P(('dom', 'feat')), may hold values from -6 to 6
Outputs:
- out_rows: bfloat16 [851968, 256], P(('dom', 'feat'))
- grad_self: float32 [128, 256], replicated
- grad_neigh: float32 [128, 256], replicated
- grad_feats: bfloat16 [128, 851968], P('feat', 'dom')
The draws below stay inside these ranges and needn't reach their ends.
Inputs may be any that keep to these rules, and one draw needn't show every extreme that they name: `adj_cols`: entry 0 of a row block names one of the partition's own 13312 / 128 blocks; entries 1 to 1 name halo slots, from 104 on. `send_list`: only the partition's first 4 blocks are ever sent. `send_count`: A partition sends nothing to itself.
All inputs are finite; a program needn't handle non-finite values.
Results may differ from the reference program's by a relative error of at most 0.0058.
Values may be sent and summed in bfloat16 or wider, within the bound.
A program may use at most 128 MiB of HBM per device.

```python
import jax
import jax.numpy as jnp
from jax import lax

F = 128
H = 256
BLK = 128
KB = 2
CAP = 2
BND = 4
ROWS_DEV = 13312
NODES = 851968
N_DOM = 64


def draw_adj_cols(key, part):
    key = jax.random.fold_in(key, 11)
    first_key, second_key = jax.random.split(key)
    row_blocks = ROWS_DEV // BLK
    block_total = N_DOM * row_blocks
    local_col = jax.random.randint(first_key, (block_total, 1), 0, row_blocks)
    halo_col = jax.random.randint(second_key, (block_total, KB - 1), row_blocks, row_blocks + N_DOM * CAP)
    columns = jnp.concatenate([local_col, halo_col], axis=1)
    columns = columns.at[0, 0].set(0).at[0, KB - 1].set(row_blocks + N_DOM * CAP - 1)
    return columns.astype(jnp.int32)


def draw_send_list(key, part):
    key = jax.random.fold_in(key, 23)
    entries = jax.random.randint(key, (N_DOM * N_DOM, CAP), 0, BND)
    entries = entries.at[0, 0].set(BND - 1).at[0, 1].set(0)
    return entries.astype(jnp.int32)


def draw_send_count(key, part):
    key = jax.random.fold_in(key, 37)
    entries = jax.random.randint(key, (N_DOM * N_DOM,), 0, CAP + 1)
    positions = jnp.arange(N_DOM * N_DOM, dtype=jnp.int32)
    sender = positions // N_DOM
    receiver = positions % N_DOM
    entries = jnp.where((sender + 1) % N_DOM == receiver, CAP, entries)
    entries = jnp.where(sender == receiver, 0, entries)
    return entries.astype(jnp.int32)


def steps_of(stream_key, shape, pieces, least, top_value):
    factor_of, own = 1.0, jax.random.fold_in(stream_key, 6)
    for dim, blocks in pieces:
        heights = jnp.exp(jax.random.uniform(jax.random.fold_in(own, dim), (blocks,), jnp.float32, least / len(pieces), top_value / len(pieces)))
        factor_of = factor_of * jnp.repeat(heights, shape[dim] // blocks).reshape([-1 if axis == dim else 1 for axis in range(len(shape))])
    return factor_of


def scatter_about(rng, shape, deviation, reach, cuts=(), held_as=jnp.bfloat16):
    array = deviation * jax.random.normal(rng, shape, jnp.float32)
    if cuts:
        array = array * steps_of(rng, shape, cuts, -0.22, 0.18)
    return jnp.clip(array, -reach, reach).astype(held_as)


def setup_inputs(seed: int = 0) -> dict:
    splits = jax.random.split(jax.random.key(seed), 9)
    return {
        "node_feats": scatter_about(splits[0], (F, NODES), 1.0, 6.0, ((0, 4), (1, 64))),
        "adj_cols": draw_adj_cols(jax.random.fold_in(splits[8], 71), 0),
        "adj_vals": scatter_about(splits[2], (NODES // BLK, KB, BLK, BLK), (KB * BLK) ** -0.5, 0.375, ((0, 64),)),
        "send_list": draw_send_list(jax.random.fold_in(splits[8], 71), 0),
        "send_count": draw_send_count(jax.random.fold_in(splits[8], 71), 0),
        "w_self": scatter_about(splits[5], (F, H), F ** -0.5, 0.5),
        "w_neigh": scatter_about(splits[6], (F, H), F ** -0.5, 0.5),
        "cotangent": scatter_about(splits[7], (NODES, H), 1.0, 6.0, ((0, 256),)),
    }


def reference(node_feats, adj_cols, adj_vals, send_list, send_count, w_self, w_neigh, cotangent):
    node_total = node_feats.shape[1]
    row_blocks = ROWS_DEV // BLK
    block_total = node_total // BLK
    blocks_all = node_feats.reshape(F, block_total, BLK).transpose(1, 0, 2)
    peer_lists = send_list.reshape(N_DOM, N_DOM, CAP)
    peer_counts = send_count.reshape(N_DOM, N_DOM)
    block_cols = adj_cols.reshape(N_DOM, row_blocks, KB)
    block_vals = adj_vals.reshape(N_DOM, row_blocks, KB, BLK, BLK)
    slot_ids = jnp.arange(CAP, dtype=jnp.int32)
    peer_ids = jnp.arange(N_DOM, dtype=jnp.int32)

    def slot_table(part_id):
        local_ids = part_id * row_blocks + jnp.arange(row_blocks, dtype=jnp.int32)
        halo_ids = (peer_ids[:, None] * row_blocks + peer_lists[:, part_id, :]).astype(jnp.int32)
        halo_live = slot_ids[None, :] < peer_counts[:, part_id][:, None]
        slot_blocks = jnp.concatenate([local_ids, halo_ids.reshape(-1)]).astype(jnp.int32)
        slot_live = jnp.concatenate([jnp.ones((row_blocks,), jnp.bool_), halo_live.reshape(-1)])
        return (slot_blocks, slot_live)

    def aggregate(part_id):
        slot_blocks, slot_live = slot_table(part_id)
        extended = blocks_all[slot_blocks].astype(jnp.float32) * slot_live[:, None, None].astype(jnp.float32)
        picked = extended[block_cols[part_id]]
        summed = jnp.einsum('rkfs,rkts->rft', picked, block_vals[part_id].astype(jnp.float32))
        return summed.astype(jnp.bfloat16)
    aggregated = lax.map(aggregate, peer_ids)
    agg_t = aggregated.transpose(2, 0, 1, 3).reshape(F, node_total)
    x_rows = node_feats.T
    agg_rows = agg_t.T
    pre = jnp.dot(x_rows, w_self, preferred_element_type=jnp.float32) + jnp.dot(agg_rows, w_neigh, preferred_element_type=jnp.float32)
    sigmoid_pre = jax.nn.sigmoid(pre)
    out_rows = (pre * sigmoid_pre).astype(jnp.bfloat16)
    grad_pre = (cotangent.astype(jnp.float32) * sigmoid_pre * (1.0 + pre * (1.0 - sigmoid_pre))).astype(jnp.bfloat16)
    norm_factor = 1.0 / jnp.sqrt(jnp.float32(node_total))
    grad_self = jnp.dot(node_feats, grad_pre, preferred_element_type=jnp.float32) * norm_factor
    grad_neigh = jnp.dot(agg_t, grad_pre, preferred_element_type=jnp.float32) * norm_factor
    dx_self = jnp.dot(grad_pre, w_self.T, preferred_element_type=jnp.float32).astype(jnp.bfloat16)
    grad_agg = jnp.dot(grad_pre, w_neigh.T, preferred_element_type=jnp.float32).astype(jnp.bfloat16)
    agg_blocks = grad_agg.T.reshape(F, block_total, BLK).transpose(1, 0, 2)

    def spread(accumulated, part_id):
        slot_blocks, slot_live = slot_table(part_id)
        own_rows = lax.dynamic_slice_in_dim(agg_blocks, (part_id * row_blocks).astype(jnp.int32), row_blocks, 0)
        terms = jnp.einsum('rft,rkts->rkfs', own_rows.astype(jnp.float32), block_vals[part_id].astype(jnp.float32))
        target = slot_blocks[block_cols[part_id]]
        live_mask = slot_live[block_cols[part_id]].astype(jnp.float32)
        terms = terms * live_mask[:, :, None, None]
        accumulated = accumulated.at[target.reshape(-1)].add(terms.reshape(-1, F, BLK))
        return (accumulated, None)
    accumulated, _ = lax.scan(spread, jnp.zeros((block_total, F, BLK), jnp.float32), peer_ids)
    grad_feats = dx_self.T.astype(jnp.float32) + accumulated.transpose(1, 0, 2).reshape(F, node_total)
    return (out_rows, grad_self, grad_neigh, grad_feats.astype(jnp.bfloat16))
```

```python
import functools
import math

import jax
import jax.numpy as jnp
from jax import lax
from jax.experimental import pallas as pl
from jax.experimental.pallas import tpu as pltpu
from jax.sharding import PartitionSpec as P

MESH = pl.DeviceIdType.MESH
F32 = jnp.float32
BF16 = jnp.bfloat16

NX, NZ, NC, NY = 4, 8, 2, 4
N_DOM = NX * NZ * NC
CAP = 2
BND = 4
BLK = 128
FL = 32
F = FL * NY
H = 256
RB = 104
RQ = RB // NY
ROWS = RQ * BLK
HALO = N_DOM * BND
JB = 3
HALO_A = N_DOM * JB
PARTS = ((0, 12), (12, 14))
CHUNK = 2 * BLK


def halo_at(c, x, z, j):
    return jnp.where(j < JB, ((c * NX + x) * NZ + z) * JB + j, HALO_A + (c * NZ + z) * NX + x)


def plan_kernel(cols, lists, counts, key, prev0, prev1, last0, last1):
    own = lax.axis_index("dom")

    def clear0(i, carry):
        last0[i] = RB
        return carry

    def clear1(i, carry):
        last1[i] = RB
        return carry

    lax.fori_loop(0, RB, clear0, 0)
    lax.fori_loop(0, HALO + 1, clear1, 0)

    def step(r, carry):
        c0 = cols[0, r]
        prev0[r] = last0[c0]
        last0[c0] = r
        slot = cols[1, r] - RB
        p = slot // CAP
        c = slot % CAP
        entry = p * N_DOM + own
        live = c < counts[entry]
        k = jnp.where(live, halo_at(p % NC, (p // NC) // NZ, (p // NC) % NZ, lists[c, entry]), HALO)
        key[r] = k
        prev1[r] = last1[k]
        last1[k] = r
        return carry

    lax.fori_loop(0, RB, step, 0)


def remote(src, dst, send_sem, recv_sem, **ids):
    return pltpu.make_async_remote_copy(
        src_ref=src, dst_ref=dst, send_sem=send_sem, recv_sem=recv_sem, device_id=ids, device_id_type=MESH
    )


def nt(a, b):
    return lax.dot_general(a, b, (((1,), (1,)), ((), ())), preferred_element_type=F32)


def layer_kernel(
    norm_factor,
    cols,
    key,
    prev0,
    prev1,
    last0,
    last1,
    x_ref,
    ws_ref,
    wn_ref,
    adj_hbm,
    cot_hbm,
    out_hbm,
    gs_ref,
    gn_ref,
    gf_ref,
    adj,
    cot,
    out,
    hal,
    xp,
    ap,
    part,
    aggt,
    gp,
    bpx,
    bpa,
    dx,
    ga,
    xb,
    terms0,
    terms1,
    hg,
    r_core,
    r_x,
    r_z,
    s_x,
    q_z,
    q_x,
    s_z,
    w_all,
    w_x,
    w_xr,
    w_zr,
    w_yr,
    w_c,
    w_cr,
    w_g,
    w_out,
    loc,
    sx,
    rx,
    sa,
    ra,
    sg,
    rg,
    sd,
    rd,
    sh,
    rh,
    sr,
    rr,
    sw,
    rw,
):
    d = lax.axis_index("dom")
    f = lax.axis_index("feat")
    c = d % NC
    z = (d // NC) % NZ
    x = d // (NC * NZ)
    oc = 1 - c

    def at_x(k):
        return lax.rem(x + k, NX)

    def at_z(k):
        return lax.rem(z + k, NZ)

    def at_y(k):
        return lax.rem(f + k, NY)

    def dom(xx, zz, cc):
        return (xx * NZ + zz) * NC + cc

    def to_x(k):
        return {"dom": dom(at_x(k), z, c)}

    def to_z(k):
        return {"dom": dom(x, at_z(k), c)}

    to_core = {"dom": dom(x, z, oc)}

    def to_y(k):
        return {"feat": at_y(k)}

    xs, zs, ys = range(1, NX), range(1, NZ), range(1, NY)

    load_adj = pltpu.make_async_copy(adj_hbm, adj, loc.at[0])
    load_adj.start()
    load_cot = pltpu.make_async_copy(cot_hbm, cot, loc.at[1])
    load_cot.start()

    barrier = pltpu.get_barrier_semaphore()
    partners = [to_x(k) for k in xs] + [to_z(k) for k in zs] + [to_y(k) for k in ys] + [to_core]
    for ids in partners:
        pl.semaphore_signal(barrier, inc=1, device_id=ids, device_id_type=MESH)

    row = c * NX + x

    def b_at(xx, zz, n):
        return pl.ds(((c * NX + xx) * NZ + zz) * JB, n * JB)

    def a_at(zz):
        return pl.ds(HALO_A + (c * NZ + zz) * NX, NX)

    for j in range(JB):
        hal[(row * NZ + z) * JB + j] = x_ref[:, j * BLK : (j + 1) * BLK]
    hal[HALO_A + (c * NZ + z) * NX + x] = x_ref[:, JB * BLK : BND * BLK]
    hal[HALO] = jnp.zeros((FL, BLK), BF16)
    terms0[RB] = jnp.zeros((FL, BLK), F32)
    terms1[RB] = jnp.zeros((FL, BLK), F32)
    pl.semaphore_wait(barrier, len(partners))

    h1z = []
    for k in zs:
        blk = hal.at[b_at(x, z, 1)]
        cp = remote(blk, blk, sh.at[k - 1], rh.at[k - 1], **to_z(k))
        cp.start()
        h1z.append(cp)
    h1x = []
    for k in xs:
        blk = hal.at[HALO_A + (c * NZ + z) * NX + x]
        cp = remote(blk, blk, sh.at[6 + k], rh.at[6 + k], **to_x(k))
        cp.start()
        h1x.append(cp)

    own_cols = pl.ds(pl.multiple_of(f * ROWS, BLK), ROWS)
    own_feats = pl.ds(pl.multiple_of(f * FL, FL), FL)
    xcp = []
    for k in ys:
        q = at_y(k)
        cp = remote(
            x_ref.at[:, pl.ds(pl.multiple_of(q * ROWS, BLK), ROWS)],
            xp.at[own_feats, :],
            sx.at[k - 1],
            rx.at[k - 1],
            **to_y(k),
        )
        cp.start()
        xcp.append(cp)
    own_x = pltpu.make_async_copy(x_ref.at[:, own_cols], xp.at[own_feats, :], loc.at[2])
    own_x.start()

    core_copies = []

    def pass_to_core(blk):
        i = 20 + len(core_copies)
        cp = remote(blk, blk, sh.at[i], rh.at[i], **to_core)
        cp.start()
        core_copies.append(cp)

    for cp in h1x:
        cp.wait()
    col3 = hal.at[a_at(z)]
    h2z = []
    for k in zs:
        cp = remote(col3, col3, sh.at[9 + k], rh.at[9 + k], **to_z(k))
        cp.start()
        h2z.append(cp)
    for cp in h1z:
        cp.wait()
    row3 = hal.at[b_at(x, 0, NZ)]
    h2x = []
    for k in xs:
        cp = remote(row3, row3, sh.at[16 + k], rh.at[16 + k], **to_x(k))
        cp.start()
        h2x.append(cp)
    pass_to_core(col3)
    pass_to_core(row3)

    def to_blocks(r, carry):
        xb[r] = x_ref[:, pl.ds(pl.multiple_of(r * BLK, BLK), BLK)]
        return carry

    lax.fori_loop(0, RB, to_blocks, 0, unroll=8)
    load_adj.wait()

    def local_part(r, carry):
        part[r] = nt(xb[cols[0, r]], adj[r, 0])
        return carry

    lax.fori_loop(0, RB, local_part, 0, unroll=8)

    for k in xs:
        h2x[k - 1].wait()
        pass_to_core(hal.at[b_at(at_x(NX - k), 0, NZ)])
    for k in zs:
        h2z[k - 1].wait()
        pass_to_core(hal.at[a_at(at_z(NZ - k))])
    for cp in core_copies:
        cp.wait()

    acp = []
    own_agg = []
    for n, (first, count) in enumerate(PARTS):
        width = count * BLK
        for k in (1, 2, 3, 0):
            q = at_y(k)
            base = q * RQ + first

            def halo_part(i, carry, base=base):
                r = base + i
                total = part[r] + nt(hal[key[r]], adj[r, 1])
                aggt[:, pl.ds(pl.multiple_of(r * BLK, BLK), BLK)] = total.astype(BF16)
                return carry

            lax.fori_loop(0, count, halo_part, 0, unroll=count // 2)
            src = aggt.at[:, pl.ds(pl.multiple_of(base * BLK, BLK), width)]
            dst = ap.at[own_feats, pl.ds(first * BLK, width)]
            if k:
                i = n * 3 + k - 1
                cp = remote(src, dst, sa.at[i], ra.at[i], **to_y(k))
                acp.append(cp)
            else:
                cp = pltpu.make_async_copy(src, dst, loc.at[3 + n])
                own_agg.append(cp)
            cp.start()

    load_cot.wait()
    own_x.wait()
    for cp in xcp:
        cp.wait()
    weights = jnp.concatenate([ws_ref[...], wn_ref[...]], axis=0)
    gcp = []
    own_g = []
    out_copies = []
    for n, (first, count) in enumerate(PARTS):
        for cp in acp[n * 3 : n * 3 + 3]:
            cp.wait()
        own_agg[n].wait()

        def products(i, carry, first=first):
            at = pl.ds(pl.multiple_of(first * BLK + i * CHUNK, CHUNK if first % 2 == 0 else BLK), CHUNK)
            panel = jnp.concatenate([xp[:, at], ap[:, at]], axis=0)
            pre = jnp.dot(panel.T, weights, preferred_element_type=F32)
            sig = 1.0 / (1.0 + jnp.exp(-pre))
            out[at, :] = (pre * sig).astype(BF16)
            g = (cot[at, :].astype(F32) * sig * (1.0 + pre * (1.0 - sig))).astype(BF16)
            gp[at, :] = g
            back = nt(weights, g).astype(BF16)
            bpx[:, at] = back[:F]
            bpa[:, at] = back[F:]
            return carry

        lax.fori_loop(0, count * BLK // CHUNK, products, 0)
        width = count * BLK
        here = pl.ds(first * BLK, width)
        there = pl.ds(pl.multiple_of(f * ROWS + first * BLK, BLK), width)
        for k in ys:
            i = n * 3 + k - 1
            cp = remote(
                bpa.at[pl.ds(pl.multiple_of(at_y(k) * FL, FL), FL), here],
                ga.at[:, there],
                sg.at[i],
                rg.at[i],
                **to_y(k),
            )
            cp.start()
            gcp.append(cp)
        cp = pltpu.make_async_copy(bpa.at[own_feats, here], ga.at[:, there], loc.at[5 + n])
        cp.start()
        own_g.append(cp)
        cp = pltpu.make_async_copy(out.at[here, :], out_hbm.at[here, :], loc.at[7 + n])
        cp.start()
        out_copies.append(cp)
    dcp = []
    for k in ys:
        cp = remote(
            bpx.at[pl.ds(pl.multiple_of(at_y(k) * FL, FL), FL), :],
            dx.at[:, own_cols],
            sd.at[k - 1],
            rd.at[k - 1],
            **to_y(k),
        )
        cp.start()
        dcp.append(cp)
    own_d = pltpu.make_async_copy(bpx.at[own_feats, :], dx.at[:, own_cols], loc.at[9])
    own_d.start()

    w_all[0:F, :] = jnp.dot(xp[...], gp[...], preferred_element_type=F32)
    w_all[F:, :] = jnp.dot(ap[...], gp[...], preferred_element_type=F32)
    step_x = 2 * F // NX
    step_z = step_x // NZ
    wcp = []
    for k in xs:
        src = w_all.at[pl.ds(pl.multiple_of(at_x(k) * step_x, step_x), step_x), :]
        cp = remote(src, w_xr.at[k - 1], sw.at[k - 1], rw.at[k - 1], **to_x(k))
        cp.start()
        wcp.append(cp)

    def terms_of(q):
        def body(i, carry):
            r = q * RQ + i
            g = ga[:, pl.ds(pl.multiple_of(r * BLK, BLK), BLK)]
            pair = jnp.concatenate([adj[r, 0], adj[r, 1]], axis=1)
            both = jnp.dot(g, pair, preferred_element_type=F32)
            terms0[r] = both[:, :BLK]
            terms1[r] = both[:, BLK:]
            return carry

        lax.fori_loop(0, RQ, body, 0, unroll=13)

    for cp in own_g:
        cp.wait()
    terms_of(f)

    for cp in wcp:
        cp.wait()
    mine = pl.ds(pl.multiple_of(x * step_x, step_x), step_x)
    w_x[...] = w_all[mine, :] + w_xr[0] + w_xr[1] + w_xr[2]
    wcp = []
    for k in zs:
        src = w_x.at[pl.ds(pl.multiple_of(at_z(k) * step_z, step_z), step_z), :]
        cp = remote(src, w_zr.at[k - 1], sw.at[2 + k], rw.at[2 + k], **to_z(k))
        cp.start()
        wcp.append(cp)

    for k in ys:
        for n in range(len(PARTS)):
            gcp[n * 3 + k - 1].wait()
        terms_of(at_y(NY - k))

    def chain(r, carry):
        terms0[r] = terms0[r] + terms0[prev0[r]]
        terms1[r] = terms1[r] + terms1[prev1[r]]
        return carry

    lax.fori_loop(0, RB, chain, 0, unroll=8)

    half_b = NX * NZ * JB
    half_a = NX * NZ

    def collect(base, n):
        def body(b, carry):
            hg[base + b] = terms1[last1[base + b]].astype(BF16)
            return carry

        lax.fori_loop(0, n, body, 0, unroll=8)

    collect(oc * half_b, half_b)
    core_b = remote(hg.at[pl.ds(oc * half_b, half_b)], r_core.at[pl.ds(0, half_b)], sr.at[0], rr.at[0], **to_core)
    core_b.start()
    collect(HALO_A + oc * half_a, half_a)
    core_a = remote(
        hg.at[pl.ds(HALO_A + oc * half_a, half_a)], r_core.at[pl.ds(half_b, half_a)], sr.at[20], rr.at[20], **to_core
    )
    core_a.start()
    collect(c * half_b, half_b)
    collect(HALO_A + c * half_a, half_a)

    for cp in wcp:
        cp.wait()
    acc = w_x[pl.ds(pl.multiple_of(z * step_z, step_z), step_z), :]
    for k in zs:
        acc = acc + w_zr[k - 1]
    w_yr[f] = acc
    wcp = []
    for k in ys:
        cp = remote(w_yr.at[f], w_yr.at[f], sw.at[9 + k], rw.at[9 + k], **to_y(k))
        cp.start()
        wcp.append(cp)

    def add_core(base, first, n):
        def body(b, carry):
            hg[base + b] = (hg[base + b].astype(F32) + r_core[first + b].astype(F32)).astype(BF16)
            return carry

        lax.fori_loop(0, n, body, 0, unroll=8)

    core_b.wait()
    add_core(c * half_b, 0, half_b)
    c1x = []
    for k in xs:
        cp = remote(hg.at[b_at(at_x(k), 0, NZ)], r_x.at[k - 1], sr.at[k], rr.at[k], **to_x(k))
        cp.start()
        c1x.append(cp)
    core_a.wait()
    add_core(HALO_A + c * half_a, half_b, half_a)
    c1z = []
    for k in zs:
        cp = remote(hg.at[a_at(at_z(k))], r_z.at[k - 1], sr.at[3 + k], rr.at[3 + k], **to_z(k))
        cp.start()
        c1z.append(cp)

    for cp in wcp:
        cp.wait()
    w_c[...] = ((w_yr[0] + w_yr[1]) + w_yr[2]) + w_yr[3]
    w_core = remote(w_c, w_cr, sw.at[13], rw.at[13], **to_core)
    w_core.start()

    for cp in c1z:
        cp.wait()
    acc = hg[a_at(z)].astype(F32)
    for k in zs:
        acc = acc + r_z[k - 1].astype(F32)
    s_z[...] = acc.astype(BF16)
    c2x = []
    for k in xs:
        cp = remote(s_z.at[at_x(k)], q_x.at[k - 1], sr.at[10 + k], rr.at[10 + k], **to_x(k))
        cp.start()
        c2x.append(cp)

    w_core.wait()
    w_g[pl.ds(pl.multiple_of(z * step_z, step_z), step_z), :] = (w_c[...] + w_cr[...]) * norm_factor
    wcp = []
    for k in zs:
        src = w_g.at[pl.ds(pl.multiple_of(z * step_z, step_z), step_z), :]
        cp = remote(src, src, sw.at[13 + k], rw.at[13 + k], **to_z(k))
        cp.start()
        wcp.append(cp)

    for cp in c1x:
        cp.wait()
    for zz in range(NZ):
        acc = hg[b_at(x, zz, 1)].astype(F32)
        for k in xs:
            acc = acc + r_x[k - 1, zz * JB : (zz + 1) * JB].astype(F32)
        s_x[zz] = acc.astype(BF16)
    c2z = []
    for k in zs:
        cp = remote(s_x.at[at_z(k)], q_z.at[k - 1], sr.at[13 + k], rr.at[13 + k], **to_z(k))
        cp.start()
        c2z.append(cp)

    for cp in wcp:
        cp.wait()
    w_out[mine, :] = w_g[...]
    wcp = []
    for k in xs:
        cp = remote(w_g, w_out.at[mine, :], sw.at[20 + k], rw.at[20 + k], **to_x(k))
        cp.start()
        wcp.append(cp)

    own_d.wait()
    for cp in dcp:
        cp.wait()

    def finish(s, carry):
        at = pl.ds(pl.multiple_of(s * BLK, BLK), BLK)
        gf_ref[:, at] = (dx[:, at].astype(F32) + terms0[last0[s]]).astype(BF16)
        return carry

    lax.fori_loop(BND, RB, finish, 0, unroll=10)
    for cp in c2x + c2z:
        cp.wait()
    for j in range(BND):
        at = pl.ds(j * BLK, BLK)
        acc = dx[:, at].astype(F32) + terms0[last0[j]]
        if j < JB:
            acc = acc + s_x[z, j].astype(F32)
            for k in zs:
                acc = acc + q_z[k - 1, j].astype(F32)
        else:
            acc = acc + s_z[x].astype(F32)
            for k in xs:
                acc = acc + q_x[k - 1].astype(F32)
        gf_ref[:, at] = acc.astype(BF16)

    for cp in wcp:
        cp.wait()
    gs_ref[...] = w_out[:F, :]
    gn_ref[...] = w_out[F:, :]
    for cp in out_copies:
        cp.wait()


def shards(node_feats, adj_cols, adj_vals, send_list, send_count, w_self, w_neigh, cotangent):
    cols = adj_cols.T
    smem = pl.BlockSpec(memory_space=pltpu.SMEM)
    vmem = pl.BlockSpec(memory_space=pltpu.VMEM)
    hbm = pl.BlockSpec(memory_space=pl.ANY)
    ints = [jax.ShapeDtypeStruct((n,), jnp.int32) for n in (RB, RB, RB, RB, HALO + 1)]
    plan = pl.pallas_call(
        plan_kernel, out_shape=ints, in_specs=[smem] * 3, out_specs=[smem] * 5, name="plan"
    )(cols, send_list.T, send_count)
    vm = pltpu.VMEM
    dma = pltpu.SemaphoreType.DMA
    step_x = 2 * F // NX
    step_z = step_x // NZ
    scratch = [
        vm((RB, 2, BLK, BLK), BF16),
        vm((ROWS, H), BF16),
        vm((ROWS, H), BF16),
        vm((HALO + 1, FL, BLK), BF16),
        vm((F, ROWS), BF16),
        vm((F, ROWS), BF16),
        vm((RB, FL, BLK), F32),
        vm((FL, RB * BLK), BF16),
        vm((ROWS, H), BF16),
        vm((F, ROWS), BF16),
        vm((F, ROWS), BF16),
        vm((FL, RB * BLK), BF16),
        vm((FL, RB * BLK), BF16),
        vm((RB, FL, BLK), BF16),
        vm((RB + 1, FL, BLK), F32),
        vm((RB + 1, FL, BLK), F32),
        vm((HALO, FL, BLK), BF16),
        vm((NX * NZ * BND, FL, BLK), BF16),
        vm((NX - 1, NZ * JB, FL, BLK), BF16),
        vm((NZ - 1, NX, FL, BLK), BF16),
        vm((NZ, JB, FL, BLK), BF16),
        vm((NZ - 1, JB, FL, BLK), BF16),
        vm((NX - 1, FL, BLK), BF16),
        vm((NX, FL, BLK), BF16),
        vm((2 * F, H), F32),
        vm((step_x, H), F32),
        vm((NX - 1, step_x, H), F32),
        vm((NZ - 1, step_z, H), F32),
        vm((NY, step_z, H), F32),
        vm((step_z, H), F32),
        vm((step_z, H), F32),
        vm((step_x, H), F32),
        vm((2 * F, H), F32),
        dma((10,)),
        dma((3,)),
        dma((3,)),
        dma((6,)),
        dma((6,)),
        dma((6,)),
        dma((6,)),
        dma((3,)),
        dma((3,)),
        dma((32,)),
        dma((32,)),
        dma((21,)),
        dma((21,)),
        dma((24,)),
        dma((24,)),
    ]
    return pl.pallas_call(
        functools.partial(layer_kernel, 1.0 / math.sqrt(RB * BLK * N_DOM)),
        out_shape=(
            jax.ShapeDtypeStruct((ROWS, H), BF16),
            jax.ShapeDtypeStruct((F, H), F32),
            jax.ShapeDtypeStruct((F, H), F32),
            jax.ShapeDtypeStruct((FL, RB * BLK), BF16),
        ),
        in_specs=[smem] * 6 + [vmem] * 3 + [hbm] * 2,
        out_specs=(hbm, vmem, vmem, vmem),
        scratch_shapes=scratch,
        compiler_params=pltpu.CompilerParams(
            collective_id=0, has_side_effects=True, vmem_limit_bytes=56 * 1024 * 1024
        ),
        cost_estimate=pl.CostEstimate(flops=1_800_000_000, bytes_accessed=14_000_000, transcendentals=852_000),
        name="layer",
    )(cols, *plan, node_feats, w_self, w_neigh, adj_vals, cotangent)


def solution(mesh):
    return jax.shard_map(
        shards,
        mesh=mesh,
        in_specs=(
            P("feat", "dom"),
            P("dom", None),
            P("dom", None, None, None),
            P(),
            P(),
            P(),
            P(),
            P(("dom", "feat"), None),
        ),
        out_specs=(P(("dom", "feat"), None), P(), P(), P("feat", "dom")),
        check_vma=False,
    )
```

```python
import functools
import math

import jax
import jax.numpy as jnp
from jax import lax
from jax.experimental import pallas as pl
from jax.experimental.pallas import tpu as pltpu
from jax.sharding import PartitionSpec as P

MESH = pl.DeviceIdType.MESH
F32 = jnp.float32
BF16 = jnp.bfloat16

NX, NZ, NC, NY = 4, 8, 2, 4
N_DOM = NX * NZ * NC
CAP = 2
BND = 4
BLK = 128
FL = 32
F = FL * NY
H = 256
RB = 104
RQ = RB // NY
ROWS = RQ * BLK
HALO = N_DOM * BND
JB = 3
HALO_A = N_DOM * JB
PARTS = ((0, 8), (8, 8), (16, 10))
CHUNK = 2 * BLK
OFFSET = (0, 1, 7, 2, 6, 3, 5, 4)
GROUPS = ((0, 1), (1, 2), (3, 2), (5, 3))


def slot_of(delta):
    return jnp.where(delta <= 4, jnp.maximum(2 * delta - 1, 0), 2 * (NZ - delta))


def make_plan(d, z, cols, lists, counts, cols_v, tab):
    lane32 = lax.broadcasted_iota(jnp.int32, (NX * NZ, BLK), 1)
    chip = lax.broadcasted_iota(jnp.int32, (NX * NZ, 1), 0)
    xx, m = chip // NZ, slot_of(lax.rem(chip % NZ - z + NZ, NZ))
    cols_v[...] = jnp.zeros_like(cols_v)
    cols_v[0:2, 0:RB] = cols[...]
    c0 = cols_v[0:1, :]
    entry = cols_v[1:2, :] - RB
    key = jnp.zeros((NX * NZ, BLK), jnp.int32)
    for core in range(NC):
        here = lane32 == core * N_DOM + d
        count = jnp.sum(jnp.where(here, counts[...], 0), axis=1, keepdims=True)
        for slot in range(CAP):
            j = jnp.sum(jnp.where(here, lists[:, slot, :], 0), axis=1, keepdims=True)
            at_b = ((core * NX + xx) * NZ + m) * JB + j
            at_a = HALO_A + (core * NZ + m) * NX + xx
            at = jnp.where(slot < count, jnp.where(j < JB, at_b, at_a), HALO)
            reads = entry == chip * (NC * CAP) + core * CAP + slot
            key = key + jnp.where(reads, at, 0)
    key = jnp.sum(key, axis=0, keepdims=True)
    r = lax.broadcasted_iota(jnp.int32, (BLK, BLK), 0)
    lane = lax.broadcasted_iota(jnp.int32, (BLK, BLK), 1)
    c0_t = jnp.broadcast_to(c0, (BLK, BLK)).T
    key_t = jnp.broadcast_to(key, (BLK, BLK)).T

    def latest(mask):
        top = jnp.max(jnp.where(mask & (r < RB), r, -1), axis=0, keepdims=True)
        return jnp.where(top < 0, RB, top)

    tab[0:1, :] = key
    tab[1:2, :] = latest((c0_t == c0) & (r < lane))
    tab[2:3, :] = latest((key_t == key) & (r < lane))
    tab[3:4, :] = latest(c0_t == lane)
    tab[4:5, :] = latest(key_t == lane)
    tab[5:6, :] = latest(key_t == lane + BLK)
    tab[6:8, :] = jnp.zeros((2, BLK), jnp.int32)


def remote(src, dst, send_sem, recv_sem, **ids):
    return pltpu.make_async_remote_copy(
        src_ref=src, dst_ref=dst, send_sem=send_sem, recv_sem=recv_sem, device_id=ids, device_id_type=MESH
    )


def nt(a, b):
    return lax.dot_general(a, b, (((1,), (1,)), ((), ())), preferred_element_type=F32)


def layer_kernel(
    norm_factor,
    cols,
    cols_ref,
    lists,
    counts,
    ws_ref,
    wn_ref,
    x_hbm,
    adj_hbm,
    cot_hbm,
    out_hbm,
    gs_ref,
    gn_ref,
    gf_ref,
    x_ref,
    adj,
    cot,
    out,
    hal,
    xp,
    ap,
    aggt,
    gp,
    bpx,
    bpa,
    dx,
    ga,
    xb,
    terms0,
    terms1,
    hg,
    r_core,
    r_x,
    r_z,
    s_x,
    q_z,
    q_x,
    s_z,
    w_all,
    w_x,
    w_xr,
    w_zr,
    w_yr,
    w_c,
    w_cr,
    w_g,
    w_out,
    cols_v,
    tab,
    plan,
    loc,
    sx,
    rx,
    sa,
    ra,
    sg,
    rg,
    sd,
    rd,
    sh,
    rh,
    sr,
    rr,
    sw,
    rw,
):
    d = lax.axis_index("dom")
    f = lax.axis_index("feat")
    c = d % NC
    z = (d // NC) % NZ
    x = d // (NC * NZ)
    oc = 1 - c

    def at_x(k):
        return lax.rem(x + k, NX)

    def at_z(k):
        return lax.rem(z + k, NZ)

    def at_y(k):
        return lax.rem(f + k, NY)

    def dom(xx, zz, cc):
        return (xx * NZ + zz) * NC + cc

    def to_x(k):
        return {"dom": dom(at_x(k), z, c)}

    def to_z(k):
        return {"dom": dom(x, at_z(k), c)}

    to_core = {"dom": dom(x, z, oc)}

    def to_y(k):
        return {"feat": at_y(k)}

    xs, zs, ys = range(1, NX), range(1, NZ), range(1, NY)

    barrier = pltpu.get_barrier_semaphore()
    partners = [to_x(k) for k in xs] + [to_z(k) for k in zs] + [to_y(k) for k in ys] + [to_core]
    for ids in partners:
        pl.semaphore_signal(barrier, inc=1, device_id=ids, device_id_type=MESH)

    own_b = (c * NX + x) * NZ * JB
    own_a = HALO_A + c * NZ * NX + x
    load_own = []
    for j in range(BND):
        at = own_b + j if j < JB else own_a
        cp = pltpu.make_async_copy(x_hbm.at[:, pl.ds(j * BLK, BLK)], hal.at[at], loc.at[11 + j])
        cp.start()
        load_own.append(cp)
    load_x = pltpu.make_async_copy(x_hbm, x_ref, loc.at[15])
    load_x.start()
    load_adj = pltpu.make_async_copy(adj_hbm, adj, loc.at[0])
    load_cot = pltpu.make_async_copy(cot_hbm, cot, loc.at[1])

    def b_at(xx, slot, n):
        return pl.ds(((c * NX + xx) * NZ + slot) * JB, n * JB)

    def a_at(slot, n=1):
        return pl.ds(HALO_A + (c * NZ + slot) * NX, n * NX)

    hal[HALO] = jnp.zeros((FL, BLK), BF16)
    terms0[RB] = jnp.zeros((FL, BLK), F32)
    terms1[RB] = jnp.zeros((FL, BLK), F32)
    for cp in load_own:
        cp.wait()
    pl.semaphore_wait(barrier, len(partners))

    def back_slot(m):
        return OFFSET.index((NZ - OFFSET[m]) % NZ)

    h1z = [None]
    for m in range(1, NZ):
        cp = remote(hal.at[b_at(x, 0, 1)], hal.at[b_at(x, back_slot(m), 1)], sh.at[m], rh.at[m], **to_z(OFFSET[m]))
        cp.start()
        h1z.append(cp)
    h1x = []
    for k in xs:
        blk = hal.at[own_a]
        cp = remote(blk, blk, sh.at[7 + k], rh.at[7 + k], **to_x(k))
        cp.start()
        h1x.append(cp)
    h2x = []

    def along_x(g):
        first, n = GROUPS[g]
        blk = hal.at[b_at(x, first, n)]
        row = []
        for k in xs:
            i = 10 + g * 3 + k
            cp = remote(blk, blk, sh.at[i], rh.at[i], **to_x(k))
            cp.start()
            row.append(cp)
        h2x.append(row)

    along_x(0)

    own_cols = pl.ds(pl.multiple_of(f * ROWS, BLK), ROWS)
    own_feats = pl.ds(pl.multiple_of(f * FL, FL), FL)
    load_x.wait()
    load_adj.start()
    xcp = []
    for k in ys:
        q = at_y(k)
        cp = remote(
            x_ref.at[:, pl.ds(pl.multiple_of(q * ROWS, BLK), ROWS)],
            xp.at[own_feats, :],
            sx.at[k - 1],
            rx.at[k - 1],
            **to_y(k),
        )
        cp.start()
        xcp.append(cp)
    own_x = pltpu.make_async_copy(x_ref.at[:, own_cols], xp.at[own_feats, :], loc.at[2])
    own_x.start()
    load_cot.start()

    core_copies = []

    def pass_to_core(at):
        i = 30 + len(core_copies)
        cp = remote(hal.at[at], hal.at[at], sh.at[i], rh.at[i], **to_core)
        cp.start()
        core_copies.append(cp)

    for cp in h1x:
        cp.wait()
    h2z = [None]
    for m in range(1, NZ):
        cp = remote(hal.at[a_at(0)], hal.at[a_at(back_slot(m))], sh.at[22 + m], rh.at[22 + m], **to_z(OFFSET[m]))
        cp.start()
        h2z.append(cp)

    make_plan(d, z, cols_ref, lists, counts, cols_v, tab)
    load_plan = pltpu.make_async_copy(tab, plan, loc.at[10])
    load_plan.start()

    def to_blocks(r, carry):
        xb[r] = x_ref[:, pl.ds(pl.multiple_of(r * BLK, BLK), BLK)]
        return carry

    for m in (1, 2):
        h1z[m].wait()
    along_x(1)
    lax.fori_loop(0, RB, to_blocks, 0, unroll=8)
    for m in (3, 4):
        h1z[m].wait()
    along_x(2)
    for m in (5, 6, 7):
        h1z[m].wait()
    along_x(3)
    pass_to_core(b_at(x, 0, NZ))
    for m in (1, 2):
        h2z[m].wait()
    pass_to_core(a_at(0, 3))
    for k in xs:
        for g in (0, 1, 2):
            h2x[g][k - 1].wait()
    for k in xs:
        pass_to_core(b_at(at_x(NX - k), 0, 5))
    for m in (3, 4):
        h2z[m].wait()
    pass_to_core(a_at(3, 2))
    load_plan.wait()
    for m in (5, 6, 7):
        h2z[m].wait()
    pass_to_core(a_at(5, 3))
    for k in xs:
        h2x[3][k - 1].wait()
        pass_to_core(b_at(at_x(NX - k), 5, 3))
    for cp in core_copies:
        cp.wait()

    load_adj.wait()
    acp = []
    own_agg = []
    for n, (first, count) in enumerate(PARTS):
        width = count * BLK
        for k in (1, 2, 3, 0):
            q = at_y(k)
            base = q * RQ + first

            def aggregate(i, carry, base=base):
                r = base + i
                sources = jnp.concatenate([xb[cols[0, r]], hal[plan[0, r]]], axis=1)
                total = nt(sources, jnp.concatenate([adj[r, 0], adj[r, 1]], axis=1))
                aggt[:, pl.ds(pl.multiple_of(r * BLK, BLK), BLK)] = total.astype(BF16)
                return carry

            lax.fori_loop(0, count, aggregate, 0, unroll=count // 2)
            src = aggt.at[:, pl.ds(pl.multiple_of(base * BLK, BLK), width)]
            dst = ap.at[own_feats, pl.ds(first * BLK, width)]
            if k:
                i = n * 3 + k - 1
                cp = remote(src, dst, sa.at[i], ra.at[i], **to_y(k))
                acp.append(cp)
            else:
                cp = pltpu.make_async_copy(src, dst, loc.at[16 + n])
                own_agg.append(cp)
            cp.start()

    load_cot.wait()
    own_x.wait()
    for cp in xcp:
        cp.wait()
    weights = jnp.concatenate([ws_ref[...], wn_ref[...]], axis=0)
    gcp = []
    own_g = []
    out_copies = []
    for n, (first, count) in enumerate(PARTS):
        for cp in acp[n * 3 : n * 3 + 3]:
            cp.wait()
        own_agg[n].wait()

        def products(i, carry, first=first):
            at = pl.ds(pl.multiple_of(first * BLK + i * CHUNK, CHUNK), CHUNK)
            panel = jnp.concatenate([xp[:, at], ap[:, at]], axis=0)
            pre = jnp.dot(panel.T, weights, preferred_element_type=F32)
            sig = 1.0 / (1.0 + jnp.exp(-pre))
            out[at, :] = (pre * sig).astype(BF16)
            g = (cot[at, :].astype(F32) * sig * (1.0 + pre * (1.0 - sig))).astype(BF16)
            gp[at, :] = g
            back = nt(weights, g).astype(BF16)
            bpx[:, at] = back[:F]
            bpa[:, at] = back[F:]
            return carry

        lax.fori_loop(0, count * BLK // CHUNK, products, 0)
        width = count * BLK
        here = pl.ds(first * BLK, width)
        there = pl.ds(pl.multiple_of(f * ROWS + first * BLK, BLK), width)
        for k in ys:
            i = n * 3 + k - 1
            cp = remote(
                bpa.at[pl.ds(pl.multiple_of(at_y(k) * FL, FL), FL), here],
                ga.at[:, there],
                sg.at[i],
                rg.at[i],
                **to_y(k),
            )
            cp.start()
            gcp.append(cp)
        cp = pltpu.make_async_copy(bpa.at[own_feats, here], ga.at[:, there], loc.at[19 + n])
        cp.start()
        own_g.append(cp)
        cp = pltpu.make_async_copy(out.at[here, :], out_hbm.at[here, :], loc.at[22 + n])
        cp.start()
        out_copies.append(cp)
    dcp = []
    for k in ys:
        cp = remote(
            bpx.at[pl.ds(pl.multiple_of(at_y(k) * FL, FL), FL), :],
            dx.at[:, own_cols],
            sd.at[k - 1],
            rd.at[k - 1],
            **to_y(k),
        )
        cp.start()
        dcp.append(cp)
    own_d = pltpu.make_async_copy(bpx.at[own_feats, :], dx.at[:, own_cols], loc.at[9])
    own_d.start()

    def add_core(base, first, n):
        def body(b, carry):
            hg[base + b] = (hg[base + b].astype(F32) + r_core[first + b].astype(F32)).astype(BF16)
            return carry

        lax.fori_loop(0, n, body, 0, unroll=8)

    w_all[0:F, :] = jnp.dot(xp[...], gp[...], preferred_element_type=F32)
    w_all[F:, :] = jnp.dot(ap[...], gp[...], preferred_element_type=F32)
    step_x = 2 * F // NX
    step_z = step_x // NZ
    wcp = []
    for k in xs:
        src = w_all.at[pl.ds(pl.multiple_of(at_x(k) * step_x, step_x), step_x), :]
        cp = remote(src, w_xr.at[k - 1], sw.at[k - 1], rw.at[k - 1], **to_x(k))
        cp.start()
        wcp.append(cp)

    def terms_of(q, first, count):
        def body(i, carry):
            r = q * RQ + first + i
            g = ga[:, pl.ds(pl.multiple_of(r * BLK, BLK), BLK)]
            pair = jnp.concatenate([adj[r, 0], adj[r, 1]], axis=1)
            both = jnp.dot(g, pair, preferred_element_type=F32)
            terms0[r] = both[:, :BLK]
            terms1[r] = both[:, BLK:]
            return carry

        lax.fori_loop(0, count, body, 0, unroll=count // 2)

    for cp in own_g:
        cp.wait()
    terms_of(f, 0, RQ)

    for cp in wcp:
        cp.wait()
    mine = pl.ds(pl.multiple_of(x * step_x, step_x), step_x)
    w_x[...] = w_all[mine, :] + w_xr[0] + w_xr[1] + w_xr[2]
    wcp = []
    for k in zs:
        src = w_x.at[pl.ds(pl.multiple_of(at_z(k) * step_z, step_z), step_z), :]
        cp = remote(src, w_zr.at[k - 1], sw.at[2 + k], rw.at[2 + k], **to_z(k))
        cp.start()
        wcp.append(cp)

    for n, (first, count) in enumerate(PARTS):
        for k in ys:
            gcp[n * 3 + k - 1].wait()
            terms_of(at_y(NY - k), first, count)

    def chain(r, carry):
        terms0[r] = terms0[r] + terms0[plan[1, r]]
        terms1[r] = terms1[r] + terms1[plan[2, r]]
        return carry

    lax.fori_loop(0, RB, chain, 0, unroll=8)

    half_b = NX * NZ * JB
    half_a = NX * NZ

    def collect(base, n):
        def body(b, carry):
            at = base + b
            hg[at] = terms1[plan[4 + at // BLK, at % BLK]].astype(BF16)
            return carry

        lax.fori_loop(0, n, body, 0, unroll=8)

    row_b = NZ * JB
    core_copies = []
    for i, k in enumerate((1, 3, 2, 0)):
        first = at_x(k) * row_b
        collect(oc * half_b + first, row_b)
        cp = remote(
            hg.at[pl.ds(oc * half_b + first, row_b)], r_core.at[pl.ds(first, row_b)], sr.at[i], rr.at[i], **to_core
        )
        cp.start()
        core_copies.append(cp)
        if i == 2:
            collect(HALO_A + oc * half_a, half_a)
            core_a = remote(
                hg.at[pl.ds(HALO_A + oc * half_a, half_a)],
                r_core.at[pl.ds(half_b, half_a)],
                sr.at[4],
                rr.at[4],
                **to_core,
            )
            core_a.start()
    collect(c * half_b, half_b)
    collect(HALO_A + c * half_a, half_a)

    for cp in wcp:
        cp.wait()
    acc = w_x[pl.ds(pl.multiple_of(z * step_z, step_z), step_z), :]
    for k in zs:
        acc = acc + w_zr[k - 1]
    w_yr[f] = acc
    wcp = []
    for k in ys:
        cp = remote(w_yr.at[f], w_yr.at[f], sw.at[9 + k], rw.at[9 + k], **to_y(k))
        cp.start()
        wcp.append(cp)

    for i, k in enumerate((1, 3, 2)):
        core_copies[i].wait()
        add_core(c * half_b + at_x(k) * row_b, at_x(k) * row_b, row_b)
    c1x = [None] * len(GROUPS)
    for g in (3, 2, 1, 0):
        first, n = GROUPS[g]
        c1x[g] = []
        for k in xs:
            i = 4 + g * 3 + k
            cp = remote(
                hg.at[b_at(at_x(k), first, n)],
                r_x.at[k - 1, pl.ds(first * JB, n * JB)],
                sr.at[i],
                rr.at[i],
                **to_x(k),
            )
            cp.start()
            c1x[g].append(cp)
    core_a.wait()
    add_core(HALO_A + c * half_a, half_b, half_a)
    c1z = []
    for m in range(1, NZ):
        cp = remote(hg.at[a_at(m)], r_z.at[m - 1], sr.at[16 + m], rr.at[16 + m], **to_z(OFFSET[m]))
        cp.start()
        c1z.append(cp)
    for cp in wcp:
        cp.wait()
    w_c[...] = ((w_yr[0] + w_yr[1]) + w_yr[2]) + w_yr[3]
    w_core = remote(w_c, w_cr, sw.at[13], rw.at[13], **to_core)
    w_core.start()

    core_copies[3].wait()
    add_core(c * half_b + x * row_b, x * row_b, row_b)
    w_core.wait()
    w_g[pl.ds(pl.multiple_of(z * step_z, step_z), step_z), :] = (w_c[...] + w_cr[...]) * norm_factor
    wcp = []
    for k in zs:
        src = w_g.at[pl.ds(pl.multiple_of(z * step_z, step_z), step_z), :]
        cp = remote(src, src, sw.at[13 + k], rw.at[13 + k], **to_z(k))
        cp.start()
        wcp.append(cp)

    c2z = []
    for g in (3, 2, 1, 0):
        for cp in c1x[g]:
            cp.wait()
        first, n = GROUPS[g]
        for m in range(first, first + n):
            at = slice(m * JB, (m + 1) * JB)
            acc = hg[b_at(x, m, 1)].astype(F32)
            for k in xs:
                acc = acc + r_x[k - 1, at].astype(F32)
            s_x[m] = acc.astype(BF16)
            if m:
                cp = remote(s_x.at[m], q_z.at[m - 1], sr.at[26 + m], rr.at[26 + m], **to_z(OFFSET[m]))
                cp.start()
                c2z.append(cp)
        if g == 2:
            for cp in c1z:
                cp.wait()
            acc = hg[a_at(0)].astype(F32)
            for k in zs:
                acc = acc + r_z[k - 1].astype(F32)
            s_z[...] = acc.astype(BF16)
            c2x = []
            for k in xs:
                cp = remote(s_z.at[at_x(k)], q_x.at[k - 1], sr.at[23 + k], rr.at[23 + k], **to_x(k))
                cp.start()
                c2x.append(cp)
        if g == 1:
            for cp in wcp:
                cp.wait()
            w_out[mine, :] = w_g[...]
            wcp = []
            for k in xs:
                cp = remote(w_g, w_out.at[mine, :], sw.at[20 + k], rw.at[20 + k], **to_x(k))
                cp.start()
                wcp.append(cp)

    own_d.wait()
    for cp in dcp:
        cp.wait()

    def finish(s, carry):
        at = pl.ds(pl.multiple_of(s * BLK, BLK), BLK)
        gf_ref[:, at] = (dx[:, at].astype(F32) + terms0[plan[3, s]]).astype(BF16)
        return carry

    lax.fori_loop(BND, RB, finish, 0, unroll=10)
    for cp in c2x + c2z:
        cp.wait()
    for j in range(BND):
        at = pl.ds(j * BLK, BLK)
        acc = dx[:, at].astype(F32) + terms0[plan[3, j]]
        if j < JB:
            acc = acc + s_x[0, j].astype(F32)
            for k in zs:
                acc = acc + q_z[k - 1, j].astype(F32)
        else:
            acc = acc + s_z[x].astype(F32)
            for k in xs:
                acc = acc + q_x[k - 1].astype(F32)
        gf_ref[:, at] = acc.astype(BF16)

    for cp in wcp:
        cp.wait()
    gs_ref[...] = w_out[:F, :]
    gn_ref[...] = w_out[F:, :]
    for cp in out_copies:
        cp.wait()


def emit_kernel(*refs):
    copies = [pltpu.make_async_copy(refs[i], refs[4 + i], refs[8].at[i]) for i in range(4)]
    for cp in copies:
        cp.start()
    for cp in copies:
        cp.wait()


def shards(node_feats, adj_cols, adj_vals, send_list, send_count, w_self, w_neigh, cotangent):
    cols = adj_cols.T
    lists = send_list.reshape(NX * NZ, NC * N_DOM, CAP).transpose(0, 2, 1)
    counts = send_count.reshape(NX * NZ, NC * N_DOM)
    smem = pl.BlockSpec(memory_space=pltpu.SMEM)
    vmem = pl.BlockSpec(memory_space=pltpu.VMEM)
    hbm = pl.BlockSpec(memory_space=pl.ANY)
    vm = pltpu.VMEM
    dma = pltpu.SemaphoreType.DMA
    step_x = 2 * F // NX
    step_z = step_x // NZ
    scratch = [
        vm((FL, RB * BLK), BF16),
        vm((RB, 2, BLK, BLK), BF16),
        vm((ROWS, H), BF16),
        vm((ROWS, H), BF16),
        vm((HALO + 1, FL, BLK), BF16),
        vm((F, ROWS), BF16),
        vm((F, ROWS), BF16),
        vm((FL, RB * BLK), BF16),
        vm((ROWS, H), BF16),
        vm((F, ROWS), BF16),
        vm((F, ROWS), BF16),
        vm((FL, RB * BLK), BF16),
        vm((FL, RB * BLK), BF16),
        vm((RB, FL, BLK), BF16),
        vm((RB + 1, FL, BLK), F32),
        vm((RB + 1, FL, BLK), F32),
        vm((HALO, FL, BLK), BF16),
        vm((NX * NZ * BND, FL, BLK), BF16),
        vm((NX - 1, NZ * JB, FL, BLK), BF16),
        vm((NZ - 1, NX, FL, BLK), BF16),
        vm((NZ, JB, FL, BLK), BF16),
        vm((NZ - 1, JB, FL, BLK), BF16),
        vm((NX - 1, FL, BLK), BF16),
        vm((NX, FL, BLK), BF16),
        vm((2 * F, H), F32),
        vm((step_x, H), F32),
        vm((NX - 1, step_x, H), F32),
        vm((NZ - 1, step_z, H), F32),
        vm((NY, step_z, H), F32),
        vm((step_z, H), F32),
        vm((step_z, H), F32),
        vm((step_x, H), F32),
        vm((2 * F, H), F32),
        vm((8, BLK), jnp.int32),
        vm((8, BLK), jnp.int32),
        pltpu.SMEM((8, BLK), jnp.int32),
        dma((25,)),
        dma((3,)),
        dma((3,)),
        dma((9,)),
        dma((9,)),
        dma((9,)),
        dma((9,)),
        dma((3,)),
        dma((3,)),
        dma((42,)),
        dma((42,)),
        dma((34,)),
        dma((34,)),
        dma((24,)),
        dma((24,)),
    ]
    results = pl.pallas_call(
        functools.partial(layer_kernel, 1.0 / math.sqrt(RB * BLK * N_DOM)),
        out_shape=(
            jax.ShapeDtypeStruct((ROWS, H), BF16),
            jax.ShapeDtypeStruct((F, H), F32),
            jax.ShapeDtypeStruct((F, H), F32),
            jax.ShapeDtypeStruct((FL, RB * BLK), BF16),
        ),
        in_specs=[smem] + [vmem] * 5 + [hbm] * 3,
        out_specs=(hbm, vmem, vmem, vmem),
        scratch_shapes=scratch,
        compiler_params=pltpu.CompilerParams(
            collective_id=0, has_side_effects=True, vmem_limit_bytes=56 * 1024 * 1024
        ),
        cost_estimate=pl.CostEstimate(flops=1_800_000_000, bytes_accessed=14_000_000, transcendentals=852_000),
        name="layer",
    )(cols, cols, lists, counts, w_self, w_neigh, node_feats, adj_vals, cotangent)
    return pl.pallas_call(
        emit_kernel,
        out_shape=[jax.ShapeDtypeStruct(a.shape, a.dtype) for a in results],
        in_specs=[vmem] * 4,
        out_specs=[hbm] * 4,
        scratch_shapes=[dma((4,))],
        name="emit",
    )(*results)


def solution(mesh):
    return jax.shard_map(
        shards,
        mesh=mesh,
        in_specs=(
            P("feat", "dom"),
            P("dom", None),
            P("dom", None, None, None),
            P(),
            P(),
            P(),
            P(),
            P(("dom", "feat"), None),
        ),
        out_specs=(P(("dom", "feat"), None), P(), P(), P("feat", "dom")),
        check_vma=False,
    )
```

```python
import functools
import math

import jax
import jax.numpy as jnp
from jax import lax
from jax.experimental import pallas as pl
from jax.experimental.pallas import tpu as pltpu
from jax.sharding import PartitionSpec as P

MESH = pl.DeviceIdType.MESH
F32 = jnp.float32
BF16 = jnp.bfloat16

NX, NZ, NC, NY = 4, 8, 2, 4
N_DOM = NX * NZ * NC
CAP = 2
BND = 4
BLK = 128
FL = 32
F = FL * NY
H = 256
RB = 104
RQ = RB // NY
ROWS = RQ * BLK
HALO = N_DOM * BND
JB = 3
HALO_A = N_DOM * JB
PARTS = ((0, 8), (8, 8), (16, 10))
CHUNK = 2 * BLK
EMIT_PARTS = 4
OFFSET = (0, 1, 7, 2, 6, 3, 5, 4)
GROUPS = ((0, 1), (1, 2), (3, 2), (5, 3))


def slot_of(delta):
    return jnp.where(delta <= 4, jnp.maximum(2 * delta - 1, 0), 2 * (NZ - delta))


def make_plan(d, z, cols, lists, counts, cols_v, tab):
    lane32 = lax.broadcasted_iota(jnp.int32, (NX * NZ, BLK), 1)
    chip = lax.broadcasted_iota(jnp.int32, (NX * NZ, 1), 0)
    xx, m = chip // NZ, slot_of(lax.rem(chip % NZ - z + NZ, NZ))
    cols_v[...] = jnp.zeros_like(cols_v)
    cols_v[0:2, 0:RB] = cols[...]
    c0 = cols_v[0:1, :]
    entry = cols_v[1:2, :] - RB
    key = jnp.zeros((NX * NZ, BLK), jnp.int32)
    for core in range(NC):
        here = lane32 == core * N_DOM + d
        count = jnp.sum(jnp.where(here, counts[...], 0), axis=1, keepdims=True)
        for slot in range(CAP):
            j = jnp.sum(jnp.where(here, lists[:, slot, :], 0), axis=1, keepdims=True)
            at_b = ((core * NX + xx) * NZ + m) * JB + j
            at_a = HALO_A + (core * NZ + m) * NX + xx
            at = jnp.where(slot < count, jnp.where(j < JB, at_b, at_a), HALO)
            reads = entry == chip * (NC * CAP) + core * CAP + slot
            key = key + jnp.where(reads, at, 0)
    key = jnp.sum(key, axis=0, keepdims=True)
    r = lax.broadcasted_iota(jnp.int32, (BLK, BLK), 0)
    lane = lax.broadcasted_iota(jnp.int32, (BLK, BLK), 1)
    c0_t = jnp.broadcast_to(c0, (BLK, BLK)).T
    key_t = jnp.broadcast_to(key, (BLK, BLK)).T

    def latest(mask):
        top = jnp.max(jnp.where(mask & (r < RB), r, -1), axis=0, keepdims=True)
        return jnp.where(top < 0, RB, top)

    tab[0:1, :] = key
    tab[1:2, :] = latest((c0_t == c0) & (r < lane))
    tab[2:3, :] = latest((key_t == key) & (r < lane))
    tab[3:4, :] = latest(c0_t == lane)
    tab[4:5, :] = latest(key_t == lane)
    tab[5:6, :] = latest(key_t == lane + BLK)
    tab[6:8, :] = jnp.zeros((2, BLK), jnp.int32)


def remote(src, dst, send_sem, recv_sem, **ids):
    return pltpu.make_async_remote_copy(
        src_ref=src, dst_ref=dst, send_sem=send_sem, recv_sem=recv_sem, device_id=ids, device_id_type=MESH
    )


def nt(a, b):
    return lax.dot_general(a, b, (((1,), (1,)), ((), ())), preferred_element_type=F32)


def layer_kernel(
    norm_factor,
    cols,
    cols_ref,
    lists_hbm,
    counts_hbm,
    ws_hbm,
    wn_hbm,
    x_hbm,
    adj_hbm,
    cot_hbm,
    out_hbm,
    gs_hbm,
    gn_hbm,
    gf_hbm,
    lists,
    counts,
    weights,
    gf_ref,
    x_ref,
    adj,
    cot,
    out,
    hal,
    xp,
    ap,
    aggt,
    gp,
    bpx,
    bpa,
    dx,
    ga,
    xb,
    terms0,
    terms1,
    hg,
    r_core,
    r_x,
    r_z,
    s_x,
    q_z,
    q_x,
    s_z,
    w_all,
    w_cr,
    w_h,
    w_x,
    w_xr,
    w_zr,
    w_yr,
    w_g,
    w_out,
    cols_v,
    tab,
    plan,
    loc,
    sx,
    rx,
    sa,
    ra,
    sg,
    rg,
    sd,
    rd,
    sh,
    rh,
    sr,
    rr,
    sw,
    rw,
):
    d = lax.axis_index("dom")
    f = lax.axis_index("feat")
    c = d % NC
    z = (d // NC) % NZ
    x = d // (NC * NZ)
    oc = 1 - c

    def at_x(k):
        return lax.rem(x + k, NX)

    def at_z(k):
        return lax.rem(z + k, NZ)

    def at_y(k):
        return lax.rem(f + k, NY)

    def dom(xx, zz, cc):
        return (xx * NZ + zz) * NC + cc

    def to_x(k):
        return {"dom": dom(at_x(k), z, c)}

    def to_z(k):
        return {"dom": dom(x, at_z(k), c)}

    to_core = {"dom": dom(x, z, oc)}

    def to_y(k):
        return {"feat": at_y(k)}

    xs, zs, ys = range(1, NX), range(1, NZ), range(1, NY)

    barrier = pltpu.get_barrier_semaphore()
    partners = [to_x(k) for k in xs] + [to_z(k) for k in zs] + [to_y(k) for k in ys] + [to_core]
    for ids in partners:
        pl.semaphore_signal(barrier, inc=1, device_id=ids, device_id_type=MESH)

    own_b = (c * NX + x) * NZ * JB
    own_a = HALO_A + c * NZ * NX + x
    load_own = []
    for j in range(BND):
        at = own_b + j if j < JB else own_a
        cp = pltpu.make_async_copy(x_hbm.at[:, pl.ds(j * BLK, BLK)], hal.at[at], loc.at[11 + j])
        cp.start()
        load_own.append(cp)
    load_x = pltpu.make_async_copy(x_hbm, x_ref, loc.at[15])
    load_x.start()
    small = []
    for i, (src, dst) in enumerate((
        (lists_hbm, lists),
        (counts_hbm, counts),
        (ws_hbm, weights.at[pl.ds(0, F), :]),
        (wn_hbm, weights.at[pl.ds(F, F), :]),
    )):
        cp = pltpu.make_async_copy(src, dst, loc.at[31 + i])
        cp.start()
        small.append(cp)
    load_adj = pltpu.make_async_copy(adj_hbm, adj, loc.at[0])
    load_cot = pltpu.make_async_copy(cot_hbm, cot, loc.at[1])

    def b_at(xx, slot, n):
        return pl.ds(((c * NX + xx) * NZ + slot) * JB, n * JB)

    def a_at(slot, n=1):
        return pl.ds(HALO_A + (c * NZ + slot) * NX, n * NX)

    hal[HALO] = jnp.zeros((FL, BLK), BF16)
    terms0[RB] = jnp.zeros((FL, BLK), F32)
    terms1[RB] = jnp.zeros((FL, BLK), F32)
    for cp in load_own:
        cp.wait()
    pl.semaphore_wait(barrier, len(partners))

    def back_slot(m):
        return OFFSET.index((NZ - OFFSET[m]) % NZ)

    h1z = [None]
    for m in range(1, NZ):
        cp = remote(hal.at[b_at(x, 0, 1)], hal.at[b_at(x, back_slot(m), 1)], sh.at[m], rh.at[m], **to_z(OFFSET[m]))
        cp.start()
        h1z.append(cp)
    h1x = []
    for k in xs:
        blk = hal.at[own_a]
        cp = remote(blk, blk, sh.at[7 + k], rh.at[7 + k], **to_x(k))
        cp.start()
        h1x.append(cp)
    h2x = []

    def along_x(g):
        first, n = GROUPS[g]
        blk = hal.at[b_at(x, first, n)]
        row = []
        for k in xs:
            i = 10 + g * 3 + k
            cp = remote(blk, blk, sh.at[i], rh.at[i], **to_x(k))
            cp.start()
            row.append(cp)
        h2x.append(row)

    along_x(0)

    own_cols = pl.ds(pl.multiple_of(f * ROWS, BLK), ROWS)
    own_feats = pl.ds(pl.multiple_of(f * FL, FL), FL)
    load_x.wait()
    load_adj.start()
    xcp = []
    for k in ys:
        q = at_y(k)
        cp = remote(
            x_ref.at[:, pl.ds(pl.multiple_of(q * ROWS, BLK), ROWS)],
            xp.at[own_feats, :],
            sx.at[k - 1],
            rx.at[k - 1],
            **to_y(k),
        )
        cp.start()
        xcp.append(cp)
    own_x = pltpu.make_async_copy(x_ref.at[:, own_cols], xp.at[own_feats, :], loc.at[2])
    own_x.start()
    load_cot.start()

    core_copies = []

    def pass_to_core(at):
        i = 30 + len(core_copies)
        cp = remote(hal.at[at], hal.at[at], sh.at[i], rh.at[i], **to_core)
        cp.start()
        core_copies.append(cp)

    for cp in h1x:
        cp.wait()
    h2z = [None]
    for m in range(1, NZ):
        cp = remote(hal.at[a_at(0)], hal.at[a_at(back_slot(m))], sh.at[22 + m], rh.at[22 + m], **to_z(OFFSET[m]))
        cp.start()
        h2z.append(cp)

    for cp in small:
        cp.wait()
    make_plan(d, z, cols_ref, lists, counts, cols_v, tab)
    load_plan = pltpu.make_async_copy(tab, plan, loc.at[10])
    load_plan.start()

    def to_blocks(r, carry):
        xb[r] = x_ref[:, pl.ds(pl.multiple_of(r * BLK, BLK), BLK)]
        return carry

    for m in (1, 2):
        h1z[m].wait()
    along_x(1)
    lax.fori_loop(0, RB, to_blocks, 0, unroll=8)
    for m in (3, 4):
        h1z[m].wait()
    along_x(2)
    for m in (5, 6, 7):
        h1z[m].wait()
    along_x(3)
    pass_to_core(b_at(x, 0, NZ))
    for m in (1, 2):
        h2z[m].wait()
    pass_to_core(a_at(0, 3))
    for k in xs:
        for g in (0, 1, 2):
            h2x[g][k - 1].wait()
    for k in xs:
        pass_to_core(b_at(at_x(NX - k), 0, 5))
    for m in (3, 4):
        h2z[m].wait()
    pass_to_core(a_at(3, 2))
    load_plan.wait()
    for m in (5, 6, 7):
        h2z[m].wait()
    pass_to_core(a_at(5, 3))
    for k in xs:
        h2x[3][k - 1].wait()
        pass_to_core(b_at(at_x(NX - k), 5, 3))
    for cp in core_copies:
        cp.wait()

    load_adj.wait()
    acp = []
    own_agg = []
    for n, (first, count) in enumerate(PARTS):
        width = count * BLK
        for k in (1, 2, 3, 0):
            q = at_y(k)
            base = q * RQ + first

            def aggregate(i, carry, base=base):
                r = base + i
                sources = jnp.concatenate([xb[cols[0, r]], hal[plan[0, r]]], axis=1)
                total = nt(sources, jnp.concatenate([adj[r, 0], adj[r, 1]], axis=1))
                aggt[:, pl.ds(pl.multiple_of(r * BLK, BLK), BLK)] = total.astype(BF16)
                return carry

            lax.fori_loop(0, count, aggregate, 0, unroll=count // 2)
            src = aggt.at[:, pl.ds(pl.multiple_of(base * BLK, BLK), width)]
            dst = ap.at[own_feats, pl.ds(first * BLK, width)]
            if k:
                i = n * 3 + k - 1
                cp = remote(src, dst, sa.at[i], ra.at[i], **to_y(k))
                acp.append(cp)
            else:
                cp = pltpu.make_async_copy(src, dst, loc.at[16 + n])
                own_agg.append(cp)
            cp.start()

    load_cot.wait()
    own_x.wait()
    for cp in xcp:
        cp.wait()
    gcp = []
    own_g = []
    out_copies = []
    for n, (first, count) in enumerate(PARTS):
        for cp in acp[n * 3 : n * 3 + 3]:
            cp.wait()
        own_agg[n].wait()

        def products(i, carry, first=first):
            at = pl.ds(pl.multiple_of(first * BLK + i * CHUNK, CHUNK), CHUNK)
            panel = jnp.concatenate([xp[:, at], ap[:, at]], axis=0)
            pre = jnp.dot(panel.T, weights[...], preferred_element_type=F32)
            sig = 1.0 / (1.0 + jnp.exp(-pre))
            out[at, :] = (pre * sig).astype(BF16)
            g = (cot[at, :].astype(F32) * sig * (1.0 + pre * (1.0 - sig))).astype(BF16)
            gp[at, :] = g
            back = nt(weights[...], g).astype(BF16)
            bpx[:, at] = back[:F]
            bpa[:, at] = back[F:]
            return carry

        lax.fori_loop(0, count * BLK // CHUNK, products, 0)
        width = count * BLK
        here = pl.ds(first * BLK, width)
        there = pl.ds(pl.multiple_of(f * ROWS + first * BLK, BLK), width)
        for k in ys:
            i = n * 3 + k - 1
            cp = remote(
                bpa.at[pl.ds(pl.multiple_of(at_y(k) * FL, FL), FL), here],
                ga.at[:, there],
                sg.at[i],
                rg.at[i],
                **to_y(k),
            )
            cp.start()
            gcp.append(cp)
        cp = pltpu.make_async_copy(bpa.at[own_feats, here], ga.at[:, there], loc.at[19 + n])
        cp.start()
        own_g.append(cp)
        cp = pltpu.make_async_copy(out.at[here, :], out_hbm.at[here, :], loc.at[22 + n])
        cp.start()
        out_copies.append(cp)
    step_x = 2 * F // NX
    step_z = step_x // NZ
    half_h = H // NC
    for i, panel in enumerate((xp, ap)):
        grad = jnp.dot(panel[...], gp[...], preferred_element_type=F32)
        for core in range(NC):
            w_all[core, i * F : (i + 1) * F, :] = grad[:, core * half_h : (core + 1) * half_h]
    mine_x = pl.ds(pl.multiple_of(x * step_x, step_x), step_x)
    mine_z = pl.ds(pl.multiple_of(z * step_z, step_z), step_z)
    w_core = remote(w_all.at[oc], w_cr, sw.at[0], rw.at[0], **to_core)
    w_core.start()

    def terms_of(q, first, count):
        def body(i, carry):
            r = q * RQ + first + i
            g = ga[:, pl.ds(pl.multiple_of(r * BLK, BLK), BLK)]
            pair = jnp.concatenate([adj[r, 0], adj[r, 1]], axis=1)
            both = jnp.dot(g, pair, preferred_element_type=F32)
            terms0[r] = both[:, :BLK]
            terms1[r] = both[:, BLK:]
            return carry

        lax.fori_loop(0, count, body, 0, unroll=count // 2)

    for cp in own_g:
        cp.wait()
    terms_of(f, 0, RQ)

    w_core.wait()
    w_h[...] = w_all[c] + w_cr[...]
    wcp = []
    for k in xs:
        src = w_h.at[pl.ds(pl.multiple_of(at_x(k) * step_x, step_x), step_x), :]
        cp = remote(src, w_xr.at[k - 1], sw.at[k], rw.at[k], **to_x(k))
        cp.start()
        wcp.append(cp)

    for n, (first, count) in enumerate(PARTS):
        for k in ys:
            gcp[n * 3 + k - 1].wait()
            terms_of(at_y(NY - k), first, count)
        if n == 1:
            for cp in wcp:
                cp.wait()
            w_x[...] = w_h[mine_x, :] + w_xr[0] + w_xr[1] + w_xr[2]
            wcp = []
            for k in zs:
                src = w_x.at[pl.ds(pl.multiple_of(at_z(k) * step_z, step_z), step_z), :]
                cp = remote(src, w_zr.at[k - 1], sw.at[3 + k], rw.at[3 + k], **to_z(k))
                cp.start()
                wcp.append(cp)

    def chain(r, carry):
        terms0[r] = terms0[r] + terms0[plan[1, r]]
        terms1[r] = terms1[r] + terms1[plan[2, r]]
        return carry

    lax.fori_loop(0, RB, chain, 0, unroll=8)

    half_b = NX * NZ * JB
    half_a = NX * NZ

    def collect(base, n):
        def body(b, carry):
            at = base + b
            hg[at] = terms1[plan[4 + at // BLK, at % BLK]].astype(BF16)
            return carry

        lax.fori_loop(0, n, body, 0, unroll=8)

    row_b = NZ * JB
    core_copies = []
    for i, k in enumerate((1, 3, 2, 0)):
        first = at_x(k) * row_b
        collect(oc * half_b + first, row_b)
        cp = remote(
            hg.at[pl.ds(oc * half_b + first, row_b)], r_core.at[pl.ds(first, row_b)], sr.at[i], rr.at[i], **to_core
        )
        cp.start()
        core_copies.append(cp)
        if i == 2:
            collect(HALO_A + oc * half_a, half_a)
            core_a = remote(
                hg.at[pl.ds(HALO_A + oc * half_a, half_a)],
                r_core.at[pl.ds(half_b, half_a)],
                sr.at[4],
                rr.at[4],
                **to_core,
            )
            core_a.start()
    collect(c * half_b, half_b)
    collect(HALO_A + c * half_a, half_a)

    for cp in wcp:
        cp.wait()
    acc = w_x[mine_z, :]
    for k in zs:
        acc = acc + w_zr[k - 1]
    w_yr[f] = acc
    wcp = []
    for k in ys:
        cp = remote(w_yr.at[f], w_yr.at[f], sw.at[10 + k], rw.at[10 + k], **to_y(k))
        cp.start()
        wcp.append(cp)

    dcp = []
    for k in ys:
        cp = remote(
            bpx.at[pl.ds(pl.multiple_of(at_y(k) * FL, FL), FL), :],
            dx.at[:, own_cols],
            sd.at[k - 1],
            rd.at[k - 1],
            **to_y(k),
        )
        cp.start()
        dcp.append(cp)
    own_d = pltpu.make_async_copy(bpx.at[own_feats, :], dx.at[:, own_cols], loc.at[9])
    own_d.start()

    def add_core(base, first, n):
        def body(b, carry):
            hg[base + b] = (hg[base + b].astype(F32) + r_core[first + b].astype(F32)).astype(BF16)
            return carry

        lax.fori_loop(0, n, body, 0, unroll=8)

    for i, k in enumerate((1, 3, 2)):
        core_copies[i].wait()
        add_core(c * half_b + at_x(k) * row_b, at_x(k) * row_b, row_b)
    c1x = [None] * len(GROUPS)
    for g in (3, 2, 1, 0):
        first, n = GROUPS[g]
        c1x[g] = []
        for k in xs:
            i = 4 + g * 3 + k
            cp = remote(
                hg.at[b_at(at_x(k), first, n)],
                r_x.at[k - 1, pl.ds(first * JB, n * JB)],
                sr.at[i],
                rr.at[i],
                **to_x(k),
            )
            cp.start()
            c1x[g].append(cp)
    core_a.wait()
    add_core(HALO_A + c * half_a, half_b, half_a)
    c1z = []
    for m in range(1, NZ):
        cp = remote(hg.at[a_at(m)], r_z.at[m - 1], sr.at[16 + m], rr.at[16 + m], **to_z(OFFSET[m]))
        cp.start()
        c1z.append(cp)
    for cp in wcp:
        cp.wait()
    w_g[mine_z, :] = (((w_yr[0] + w_yr[1]) + w_yr[2]) + w_yr[3]) * norm_factor
    wcp = []
    for k in zs:
        cp = remote(w_g.at[mine_z, :], w_g.at[mine_z, :], sw.at[13 + k], rw.at[13 + k], **to_z(k))
        cp.start()
        wcp.append(cp)

    core_copies[3].wait()
    add_core(c * half_b + x * row_b, x * row_b, row_b)
    c2z = []
    for g in (3, 2, 1, 0):
        for cp in c1x[g]:
            cp.wait()
        first, n = GROUPS[g]
        for m in range(first, first + n):
            at = slice(m * JB, (m + 1) * JB)
            acc = hg[b_at(x, m, 1)].astype(F32)
            for k in xs:
                acc = acc + r_x[k - 1, at].astype(F32)
            s_x[m] = acc.astype(BF16)
            if m:
                cp = remote(s_x.at[m], q_z.at[m - 1], sr.at[26 + m], rr.at[26 + m], **to_z(OFFSET[m]))
                cp.start()
                c2z.append(cp)
        if g == 2:
            for cp in c1z:
                cp.wait()
            acc = hg[a_at(0)].astype(F32)
            for k in zs:
                acc = acc + r_z[k - 1].astype(F32)
            s_z[...] = acc.astype(BF16)
            c2x = []
            for k in xs:
                cp = remote(s_z.at[at_x(k)], q_x.at[k - 1], sr.at[23 + k], rr.at[23 + k], **to_x(k))
                cp.start()
                c2x.append(cp)
        if g == 3:
            for cp in wcp:
                cp.wait()
            w_out[c, mine_x, :] = w_g[...]
            wcp = []
            for k in xs:
                cp = remote(w_g, w_out.at[c, mine_x, :], sw.at[20 + k], rw.at[20 + k], **to_x(k))
                cp.start()
                wcp.append(cp)

        if g == 0:
            for cp in wcp:
                cp.wait()
            w_core = remote(w_out.at[c], w_out.at[c], sw.at[24], rw.at[24], **to_core)
            w_core.start()

    own_d.wait()
    for cp in dcp:
        cp.wait()

    def finish(s, carry):
        at = pl.ds(pl.multiple_of(s * BLK, BLK), BLK)
        gf_ref[:, at] = (dx[:, at].astype(F32) + terms0[plan[3, s]]).astype(BF16)
        return carry

    lax.fori_loop(BND, RB, finish, 0, unroll=10)
    tail = pl.ds(BND * BLK, (RB - BND) * BLK)
    put_tail = pltpu.make_async_copy(gf_ref.at[:, tail], gf_hbm.at[:, tail], loc.at[25])
    put_tail.start()
    for cp in c2x + c2z:
        cp.wait()
    for j in range(BND):
        at = pl.ds(j * BLK, BLK)
        acc = dx[:, at].astype(F32) + terms0[plan[3, j]]
        if j < JB:
            acc = acc + s_x[0, j].astype(F32)
            for k in zs:
                acc = acc + q_z[k - 1, j].astype(F32)
        else:
            acc = acc + s_z[x].astype(F32)
            for k in xs:
                acc = acc + q_x[k - 1].astype(F32)
        gf_ref[:, at] = acc.astype(BF16)

    head = pl.ds(0, BND * BLK)
    put_head = pltpu.make_async_copy(gf_ref.at[:, head], gf_hbm.at[:, head], loc.at[26])
    put_head.start()

    w_core.wait()
    puts = []
    for core in range(NC):
        for i, dst in enumerate((gs_hbm, gn_hbm)):
            cp = pltpu.make_async_copy(
                w_out.at[core, pl.ds(i * F, F), :],
                dst.at[:, pl.ds(core * half_h, half_h)],
                loc.at[27 + 2 * core + i],
            )
            cp.start()
            puts.append(cp)
    for cp in out_copies + puts + [put_tail, put_head]:
        cp.wait()


def emit_kernel(*refs):
    sems = refs[12]
    pieces = []
    for src, dst, held in zip(refs[:4], refs[4:8], refs[8:12]):
        parts = EMIT_PARTS if src.shape[0] * src.shape[1] > 2 * F * H else 1
        rows = src.shape[0] // parts
        for p in range(parts):
            at = pl.ds(p * rows, rows)
            n = 2 * len(pieces)
            into = pltpu.make_async_copy(src.at[at, :], held.at[at, :], sems.at[n])
            into.start()
            pieces.append((into, pltpu.make_async_copy(held.at[at, :], dst.at[at, :], sems.at[n + 1])))
    for into, out in pieces:
        into.wait()
        out.start()
    for _, out in pieces:
        out.wait()


def shards(node_feats, adj_cols, adj_vals, send_list, send_count, w_self, w_neigh, cotangent):
    cols = adj_cols.T
    lists = send_list.reshape(NX * NZ, NC * N_DOM, CAP).transpose(0, 2, 1)
    counts = send_count.reshape(NX * NZ, NC * N_DOM)
    smem = pl.BlockSpec(memory_space=pltpu.SMEM)
    vmem = pl.BlockSpec(memory_space=pltpu.VMEM)
    hbm = pl.BlockSpec(memory_space=pl.ANY)
    vm = pltpu.VMEM
    dma = pltpu.SemaphoreType.DMA
    half_h = H // NC
    step_x = 2 * F // NX
    step_z = step_x // NZ
    scratch = [
        vm((NX * NZ, CAP, NC * N_DOM), jnp.int32),
        vm((NX * NZ, NC * N_DOM), jnp.int32),
        vm((2 * F, H), BF16),
        vm((FL, RB * BLK), BF16),
        vm((FL, RB * BLK), BF16),
        vm((RB, 2, BLK, BLK), BF16),
        vm((ROWS, H), BF16),
        vm((ROWS, H), BF16),
        vm((HALO + 1, FL, BLK), BF16),
        vm((F, ROWS), BF16),
        vm((F, ROWS), BF16),
        vm((FL, RB * BLK), BF16),
        vm((ROWS, H), BF16),
        vm((F, ROWS), BF16),
        vm((F, ROWS), BF16),
        vm((FL, RB * BLK), BF16),
        vm((FL, RB * BLK), BF16),
        vm((RB, FL, BLK), BF16),
        vm((RB + 1, FL, BLK), F32),
        vm((RB + 1, FL, BLK), F32),
        vm((HALO, FL, BLK), BF16),
        vm((NX * NZ * BND, FL, BLK), BF16),
        vm((NX - 1, NZ * JB, FL, BLK), BF16),
        vm((NZ - 1, NX, FL, BLK), BF16),
        vm((NZ, JB, FL, BLK), BF16),
        vm((NZ - 1, JB, FL, BLK), BF16),
        vm((NX - 1, FL, BLK), BF16),
        vm((NX, FL, BLK), BF16),
        vm((NC, 2 * F, half_h), F32),
        vm((2 * F, half_h), F32),
        vm((2 * F, half_h), F32),
        vm((step_x, half_h), F32),
        vm((NX - 1, step_x, half_h), F32),
        vm((NZ - 1, step_z, half_h), F32),
        vm((NY, step_z, half_h), F32),
        vm((step_x, half_h), F32),
        vm((NC, 2 * F, half_h), F32),
        vm((8, BLK), jnp.int32),
        vm((8, BLK), jnp.int32),
        pltpu.SMEM((8, BLK), jnp.int32),
        dma((35,)),
        dma((3,)),
        dma((3,)),
        dma((9,)),
        dma((9,)),
        dma((9,)),
        dma((9,)),
        dma((3,)),
        dma((3,)),
        dma((42,)),
        dma((42,)),
        dma((34,)),
        dma((34,)),
        dma((25,)),
        dma((25,)),
    ]
    results = pl.pallas_call(
        functools.partial(layer_kernel, 1.0 / math.sqrt(RB * BLK * N_DOM)),
        out_shape=(
            jax.ShapeDtypeStruct((ROWS, H), BF16),
            jax.ShapeDtypeStruct((F, H), F32),
            jax.ShapeDtypeStruct((F, H), F32),
            jax.ShapeDtypeStruct((FL, RB * BLK), BF16),
        ),
        in_specs=[smem, vmem] + [hbm] * 7,
        out_specs=(hbm, hbm, hbm, hbm),
        scratch_shapes=scratch,
        compiler_params=pltpu.CompilerParams(
            collective_id=0, has_side_effects=True, vmem_limit_bytes=56 * 1024 * 1024
        ),
        cost_estimate=pl.CostEstimate(flops=1_800_000_000, bytes_accessed=14_000_000, transcendentals=852_000),
        name="layer",
    )(cols, cols, lists, counts, w_self, w_neigh, node_feats, adj_vals, cotangent)
    return pl.pallas_call(
        emit_kernel,
        out_shape=[jax.ShapeDtypeStruct(a.shape, a.dtype) for a in results],
        in_specs=[hbm] * 4,
        out_specs=[hbm] * 4,
        scratch_shapes=[vm(a.shape, a.dtype) for a in results] + [dma((4 * EMIT_PARTS + 4,))],
        compiler_params=pltpu.CompilerParams(vmem_limit_bytes=56 * 1024 * 1024),
        name="emit",
    )(*results)


def solution(mesh):
    return jax.shard_map(
        shards,
        mesh=mesh,
        in_specs=(
            P("feat", "dom"),
            P("dom", None),
            P("dom", None, None, None),
            P(),
            P(),
            P(),
            P(),
            P(("dom", "feat"), None),
        ),
        out_specs=(P(("dom", "feat"), None), P(), P(), P("feat", "dom")),
        check_vma=False,
    )
```

```python
import functools
import math

import jax
import jax.numpy as jnp
from jax import lax
from jax.experimental import pallas as pl
from jax.experimental.pallas import tpu as pltpu
from jax.sharding import PartitionSpec as P

MESH = pl.DeviceIdType.MESH
F32 = jnp.float32
BF16 = jnp.bfloat16

NX, NZ, NC, NY = 4, 8, 2, 4
N_DOM = NX * NZ * NC
CAP = 2
BND = 4
BLK = 128
FL = 32
F = FL * NY
H = 256
RB = 104
RQ = RB // NY
ROWS = RQ * BLK
HALO = N_DOM * BND
JB = 3
HALO_A = N_DOM * JB
PARTS = ((0, 8), (8, 8), (16, 10))
CHUNK = 2 * BLK
EMIT_PARTS = 4
OFFSET = (0, 1, 7, 2, 6, 3, 5, 4)
GROUPS = ((0, 1), (1, 2), (3, 2), (5, 3))


def slot_of(delta):
    return jnp.where(delta <= 4, jnp.maximum(2 * delta - 1, 0), 2 * (NZ - delta))


def make_plan(d, z, cols, lists, counts, cols_v, tab):
    lane32 = lax.broadcasted_iota(jnp.int32, (NX * NZ, BLK), 1)
    chip = lax.broadcasted_iota(jnp.int32, (NX * NZ, 1), 0)
    xx, m = chip // NZ, slot_of(lax.rem(chip % NZ - z + NZ, NZ))
    cols_v[...] = jnp.zeros_like(cols_v)
    cols_v[0:2, 0:RB] = cols[...]
    c0 = cols_v[0:1, :]
    entry = cols_v[1:2, :] - RB
    key = jnp.zeros((NX * NZ, BLK), jnp.int32)
    for core in range(NC):
        here = lane32 == core * N_DOM + d
        count = jnp.sum(jnp.where(here, counts[...], 0), axis=1, keepdims=True)
        for slot in range(CAP):
            j = jnp.sum(jnp.where(here, lists[:, slot, :], 0), axis=1, keepdims=True)
            at_b = ((core * NX + xx) * NZ + m) * JB + j
            at_a = HALO_A + (core * NZ + m) * NX + xx
            at = jnp.where(slot < count, jnp.where(j < JB, at_b, at_a), HALO)
            reads = entry == chip * (NC * CAP) + core * CAP + slot
            key = key + jnp.where(reads, at, 0)
    key = jnp.sum(key, axis=0, keepdims=True)
    r = lax.broadcasted_iota(jnp.int32, (BLK, BLK), 0)
    lane = lax.broadcasted_iota(jnp.int32, (BLK, BLK), 1)
    c0_t = jnp.broadcast_to(c0, (BLK, BLK)).T
    key_t = jnp.broadcast_to(key, (BLK, BLK)).T

    def latest(mask):
        top = jnp.max(jnp.where(mask & (r < RB), r, -1), axis=0, keepdims=True)
        return jnp.where(top < 0, RB, top)

    tab[0:1, :] = key
    tab[1:2, :] = latest((c0_t == c0) & (r < lane))
    tab[2:3, :] = latest((key_t == key) & (r < lane))
    tab[3:4, :] = latest(c0_t == lane)
    tab[4:5, :] = latest(key_t == lane)
    tab[5:6, :] = latest(key_t == lane + BLK)
    tab[6:8, :] = jnp.zeros((2, BLK), jnp.int32)


def remote(src, dst, send_sem, recv_sem, **ids):
    return pltpu.make_async_remote_copy(
        src_ref=src, dst_ref=dst, send_sem=send_sem, recv_sem=recv_sem, device_id=ids, device_id_type=MESH
    )


def nt(a, b):
    return lax.dot_general(a, b, (((1,), (1,)), ((), ())), preferred_element_type=F32)


def layer_kernel(
    norm_factor,
    cols,
    cols_ref,
    lists_hbm,
    counts_hbm,
    ws_hbm,
    wn_hbm,
    x_hbm,
    adj_hbm,
    cot_hbm,
    out_hbm,
    gs_hbm,
    gn_hbm,
    gf_hbm,
    lists,
    counts,
    weights,
    gf_ref,
    x_ref,
    adj,
    cot,
    out,
    hal,
    xp,
    ap,
    aggt,
    gp,
    bpx,
    bpa,
    dx,
    ga,
    xb,
    terms0,
    terms1,
    hg,
    r_core,
    r_x,
    r_z,
    s_x,
    q_z,
    q_x,
    s_z,
    w_all,
    w_cr,
    w_h,
    w_x,
    w_xr,
    w_zr,
    w_yr,
    w_g,
    w_out,
    cols_v,
    tab,
    plan,
    loc,
    sx,
    rx,
    sa,
    ra,
    sg,
    rg,
    sd,
    rd,
    sh,
    rh,
    sr,
    rr,
    sw,
    rw,
):
    d = lax.axis_index("dom")
    f = lax.axis_index("feat")
    c = d % NC
    z = (d // NC) % NZ
    x = d // (NC * NZ)
    oc = 1 - c

    def at_x(k):
        return lax.rem(x + k, NX)

    def at_z(k):
        return lax.rem(z + k, NZ)

    def at_y(k):
        return lax.rem(f + k, NY)

    def dom(xx, zz, cc):
        return (xx * NZ + zz) * NC + cc

    def to_x(k):
        return {"dom": dom(at_x(k), z, c)}

    def to_z(k):
        return {"dom": dom(x, at_z(k), c)}

    to_core = {"dom": dom(x, z, oc)}

    def to_y(k):
        return {"feat": at_y(k)}

    xs, zs, ys = range(1, NX), range(1, NZ), range(1, NY)

    barrier = pltpu.get_barrier_semaphore()
    partners = [to_x(k) for k in xs] + [to_z(k) for k in zs] + [to_y(k) for k in ys] + [to_core]
    for ids in partners:
        pl.semaphore_signal(barrier, inc=1, device_id=ids, device_id_type=MESH)

    own_b = (c * NX + x) * NZ * JB
    own_a = HALO_A + c * NZ * NX + x
    load_own = []
    for j in range(BND):
        at = own_b + j if j < JB else own_a
        cp = pltpu.make_async_copy(x_hbm.at[:, pl.ds(j * BLK, BLK)], hal.at[at], loc.at[11 + j])
        cp.start()
        load_own.append(cp)
    load_x = pltpu.make_async_copy(x_hbm, x_ref, loc.at[15])
    load_x.start()
    small = []
    for i, (src, dst) in enumerate((
        (lists_hbm, lists),
        (counts_hbm, counts),
        (ws_hbm, weights.at[pl.ds(0, F), :]),
        (wn_hbm, weights.at[pl.ds(F, F), :]),
    )):
        cp = pltpu.make_async_copy(src, dst, loc.at[31 + i])
        cp.start()
        small.append(cp)
    load_adj = pltpu.make_async_copy(adj_hbm, adj, loc.at[0])
    load_cot = pltpu.make_async_copy(cot_hbm, cot, loc.at[1])

    def b_at(xx, slot, n):
        return pl.ds(((c * NX + xx) * NZ + slot) * JB, n * JB)

    def a_at(slot, n=1):
        return pl.ds(HALO_A + (c * NZ + slot) * NX, n * NX)

    hal[HALO] = jnp.zeros((FL, BLK), BF16)
    terms0[RB] = jnp.zeros((FL, BLK), F32)
    terms1[RB] = jnp.zeros((FL, BLK), F32)
    for cp in load_own:
        cp.wait()
    pl.semaphore_wait(barrier, len(partners))

    def back_slot(m):
        return OFFSET.index((NZ - OFFSET[m]) % NZ)

    h1z = [None]
    for m in range(1, NZ):
        cp = remote(hal.at[b_at(x, 0, 1)], hal.at[b_at(x, back_slot(m), 1)], sh.at[m], rh.at[m], **to_z(OFFSET[m]))
        cp.start()
        h1z.append(cp)
    h1x = []
    for k in xs:
        blk = hal.at[own_a]
        cp = remote(blk, blk, sh.at[7 + k], rh.at[7 + k], **to_x(k))
        cp.start()
        h1x.append(cp)
    h2x = []

    def along_x(g):
        first, n = GROUPS[g]
        blk = hal.at[b_at(x, first, n)]
        row = []
        for k in xs:
            i = 10 + g * 3 + k
            cp = remote(blk, blk, sh.at[i], rh.at[i], **to_x(k))
            cp.start()
            row.append(cp)
        h2x.append(row)

    along_x(0)

    own_cols = pl.ds(pl.multiple_of(f * ROWS, BLK), ROWS)
    own_feats = pl.ds(pl.multiple_of(f * FL, FL), FL)
    load_x.wait()
    load_adj.start()
    xcp = []
    for k in ys:
        q = at_y(k)
        cp = remote(
            x_ref.at[:, pl.ds(pl.multiple_of(q * ROWS, BLK), ROWS)],
            xp.at[own_feats, :],
            sx.at[k - 1],
            rx.at[k - 1],
            **to_y(k),
        )
        cp.start()
        xcp.append(cp)
    own_x = pltpu.make_async_copy(x_ref.at[:, own_cols], xp.at[own_feats, :], loc.at[2])
    own_x.start()
    load_cot.start()

    core_copies = []

    def pass_to_core(at):
        i = 30 + len(core_copies)
        cp = remote(hal.at[at], hal.at[at], sh.at[i], rh.at[i], **to_core)
        cp.start()
        core_copies.append(cp)

    for cp in h1x:
        cp.wait()
    h2z = [None]
    for m in range(1, NZ):
        cp = remote(hal.at[a_at(0)], hal.at[a_at(back_slot(m))], sh.at[22 + m], rh.at[22 + m], **to_z(OFFSET[m]))
        cp.start()
        h2z.append(cp)

    for cp in small:
        cp.wait()
    make_plan(d, z, cols_ref, lists, counts, cols_v, tab)
    load_plan = pltpu.make_async_copy(tab, plan, loc.at[10])
    load_plan.start()

    def to_blocks(r, carry):
        xb[r] = x_ref[:, pl.ds(pl.multiple_of(r * BLK, BLK), BLK)]
        return carry

    for m in (1, 2):
        h1z[m].wait()
    along_x(1)
    lax.fori_loop(0, RB, to_blocks, 0, unroll=8)
    for m in (3, 4):
        h1z[m].wait()
    along_x(2)
    for m in (5, 6, 7):
        h1z[m].wait()
    along_x(3)
    pass_to_core(b_at(x, 0, NZ))
    for m in (1, 2):
        h2z[m].wait()
    pass_to_core(a_at(0, 3))
    for k in xs:
        for g in (0, 1, 2):
            h2x[g][k - 1].wait()
    for k in xs:
        pass_to_core(b_at(at_x(NX - k), 0, 5))
    for m in (3, 4):
        h2z[m].wait()
    pass_to_core(a_at(3, 2))
    load_plan.wait()
    for m in (5, 6, 7):
        h2z[m].wait()
    pass_to_core(a_at(5, 3))
    for k in xs:
        h2x[3][k - 1].wait()
        pass_to_core(b_at(at_x(NX - k), 5, 3))
    for cp in core_copies:
        cp.wait()

    load_adj.wait()
    acp = []
    own_agg = []
    for n, (first, count) in enumerate(PARTS):
        width = count * BLK
        for k in (1, 2, 3, 0):
            q = at_y(k)
            base = q * RQ + first

            def aggregate(i, carry, base=base):
                r = base + i
                sources = jnp.concatenate([xb[cols[0, r]], hal[plan[0, r]]], axis=1)
                total = nt(sources, jnp.concatenate([adj[r, 0], adj[r, 1]], axis=1))
                aggt[:, pl.ds(pl.multiple_of(r * BLK, BLK), BLK)] = total.astype(BF16)
                return carry

            lax.fori_loop(0, count, aggregate, 0, unroll=count // 2)
            src = aggt.at[:, pl.ds(pl.multiple_of(base * BLK, BLK), width)]
            dst = ap.at[own_feats, pl.ds(first * BLK, width)]
            if k:
                i = n * 3 + k - 1
                cp = remote(src, dst, sa.at[i], ra.at[i], **to_y(k))
                acp.append(cp)
            else:
                cp = pltpu.make_async_copy(src, dst, loc.at[16 + n])
                own_agg.append(cp)
            cp.start()

    load_cot.wait()
    own_x.wait()
    for cp in xcp:
        cp.wait()
    gcp = []
    own_g = []
    out_copies = []
    for n, (first, count) in enumerate(PARTS):
        for cp in acp[n * 3 : n * 3 + 3]:
            cp.wait()
        own_agg[n].wait()

        def products(i, carry, first=first):
            at = pl.ds(pl.multiple_of(first * BLK + i * CHUNK, CHUNK), CHUNK)
            panel = jnp.concatenate([xp[:, at], ap[:, at]], axis=0)
            pre = jnp.dot(panel.T, weights[...], preferred_element_type=F32)
            sig = 1.0 / (1.0 + jnp.exp(-pre))
            out[at, :] = (pre * sig).astype(BF16)
            g = (cot[at, :].astype(F32) * sig * (1.0 + pre * (1.0 - sig))).astype(BF16)
            gp[at, :] = g
            back = nt(weights[...], g).astype(BF16)
            bpx[:, at] = back[:F]
            bpa[:, at] = back[F:]
            return carry

        lax.fori_loop(0, count * BLK // CHUNK, products, 0)
        width = count * BLK
        here = pl.ds(first * BLK, width)
        there = pl.ds(pl.multiple_of(f * ROWS + first * BLK, BLK), width)
        for k in ys:
            i = n * 3 + k - 1
            cp = remote(
                bpa.at[pl.ds(pl.multiple_of(at_y(k) * FL, FL), FL), here],
                ga.at[:, there],
                sg.at[i],
                rg.at[i],
                **to_y(k),
            )
            cp.start()
            gcp.append(cp)
        cp = pltpu.make_async_copy(bpa.at[own_feats, here], ga.at[:, there], loc.at[19 + n])
        cp.start()
        own_g.append(cp)
        cp = pltpu.make_async_copy(out.at[here, :], out_hbm.at[here, :], loc.at[22 + n])
        cp.start()
        out_copies.append(cp)
    step_x = 2 * F // NX
    step_z = step_x // NZ
    half_h = H // NC
    for i, panel in enumerate((xp, ap)):
        grad = jnp.dot(panel[...], gp[...], preferred_element_type=F32)
        for core in range(NC):
            w_all[core, i * F : (i + 1) * F, :] = grad[:, core * half_h : (core + 1) * half_h]
    mine_x = pl.ds(pl.multiple_of(x * step_x, step_x), step_x)
    mine_z = pl.ds(pl.multiple_of(z * step_z, step_z), step_z)
    w_core = remote(w_all.at[oc], w_cr, sw.at[0], rw.at[0], **to_core)
    w_core.start()

    def terms_of(q, first, count):
        def body(i, carry):
            r = q * RQ + first + i
            g = ga[:, pl.ds(pl.multiple_of(r * BLK, BLK), BLK)]
            pair = jnp.concatenate([adj[r, 0], adj[r, 1]], axis=1)
            both = jnp.dot(g, pair, preferred_element_type=F32)
            terms0[r] = both[:, :BLK]
            terms1[r] = both[:, BLK:]
            return carry

        lax.fori_loop(0, count, body, 0, unroll=count // 2)

    for cp in own_g:
        cp.wait()
    terms_of(f, 0, RQ)

    w_core.wait()
    w_h[...] = w_all[c] + w_cr[...]
    wcp = []
    for k in xs:
        src = w_h.at[pl.ds(pl.multiple_of(at_x(k) * step_x, step_x), step_x), :]
        cp = remote(src, w_xr.at[k - 1], sw.at[k], rw.at[k], **to_x(k))
        cp.start()
        wcp.append(cp)

    for n, (first, count) in enumerate(PARTS):
        for k in ys:
            gcp[n * 3 + k - 1].wait()
            terms_of(at_y(NY - k), first, count)
        if n == 1:
            for cp in wcp:
                cp.wait()
            w_x[...] = w_h[mine_x, :] + w_xr[0] + w_xr[1] + w_xr[2]
            wcp = []
            for k in zs:
                src = w_x.at[pl.ds(pl.multiple_of(at_z(k) * step_z, step_z), step_z), :]
                cp = remote(src, w_zr.at[k - 1], sw.at[3 + k], rw.at[3 + k], **to_z(k))
                cp.start()
                wcp.append(cp)

    def chain(r, carry):
        terms0[r] = terms0[r] + terms0[plan[1, r]]
        terms1[r] = terms1[r] + terms1[plan[2, r]]
        return carry

    lax.fori_loop(0, RB, chain, 0, unroll=8)

    half_b = NX * NZ * JB
    half_a = NX * NZ

    def collect(base, n):
        def body(b, carry):
            at = base + b
            hg[at] = terms1[plan[4 + at // BLK, at % BLK]].astype(BF16)
            return carry

        lax.fori_loop(0, n, body, 0, unroll=8)

    row_b = NZ * JB
    core_copies = []
    for i, k in enumerate((1, 3, 2, 0)):
        first = at_x(k) * row_b
        collect(oc * half_b + first, row_b)
        cp = remote(
            hg.at[pl.ds(oc * half_b + first, row_b)], r_core.at[pl.ds(first, row_b)], sr.at[i], rr.at[i], **to_core
        )
        cp.start()
        core_copies.append(cp)
        if i == 2:
            collect(HALO_A + oc * half_a, half_a)
            core_a = remote(
                hg.at[pl.ds(HALO_A + oc * half_a, half_a)],
                r_core.at[pl.ds(half_b, half_a)],
                sr.at[4],
                rr.at[4],
                **to_core,
            )
            core_a.start()
    collect(c * half_b, half_b)
    collect(HALO_A + c * half_a, half_a)

    for cp in wcp:
        cp.wait()
    acc = w_x[mine_z, :]
    for k in zs:
        acc = acc + w_zr[k - 1]
    w_yr[f] = acc
    wcp = []
    for k in ys:
        cp = remote(w_yr.at[f], w_yr.at[f], sw.at[10 + k], rw.at[10 + k], **to_y(k))
        cp.start()
        wcp.append(cp)

    dcp = []
    for k in ys:
        cp = remote(
            bpx.at[pl.ds(pl.multiple_of(at_y(k) * FL, FL), FL), :],
            dx.at[:, own_cols],
            sd.at[k - 1],
            rd.at[k - 1],
            **to_y(k),
        )
        cp.start()
        dcp.append(cp)
    own_d = pltpu.make_async_copy(bpx.at[own_feats, :], dx.at[:, own_cols], loc.at[9])
    own_d.start()

    def add_core(base, first, n):
        def body(b, carry):
            hg[base + b] = (hg[base + b].astype(F32) + r_core[first + b].astype(F32)).astype(BF16)
            return carry

        lax.fori_loop(0, n, body, 0, unroll=8)

    for i, k in enumerate((1, 3, 2)):
        core_copies[i].wait()
        add_core(c * half_b + at_x(k) * row_b, at_x(k) * row_b, row_b)
    c1x = [None] * len(GROUPS)
    for g in (3, 2, 1, 0):
        first, n = GROUPS[g]
        c1x[g] = []
        for k in xs:
            i = 4 + g * 3 + k
            cp = remote(
                hg.at[b_at(at_x(k), first, n)],
                r_x.at[k - 1, pl.ds(first * JB, n * JB)],
                sr.at[i],
                rr.at[i],
                **to_x(k),
            )
            cp.start()
            c1x[g].append(cp)
    core_a.wait()
    add_core(HALO_A + c * half_a, half_b, half_a)
    c1z = []
    for m in range(1, NZ):
        cp = remote(hg.at[a_at(m)], r_z.at[m - 1], sr.at[16 + m], rr.at[16 + m], **to_z(OFFSET[m]))
        cp.start()
        c1z.append(cp)
    for cp in wcp:
        cp.wait()
    w_g[mine_z, :] = (((w_yr[0] + w_yr[1]) + w_yr[2]) + w_yr[3]) * norm_factor
    wcp = []
    for k in zs:
        cp = remote(w_g.at[mine_z, :], w_g.at[mine_z, :], sw.at[13 + k], rw.at[13 + k], **to_z(k))
        cp.start()
        wcp.append(cp)

    core_copies[3].wait()
    add_core(c * half_b + x * row_b, x * row_b, row_b)
    c2z = []
    for g in (3, 2, 1, 0):
        for cp in c1x[g]:
            cp.wait()
        first, n = GROUPS[g]
        for m in range(first, first + n):
            at = slice(m * JB, (m + 1) * JB)
            acc = hg[b_at(x, m, 1)].astype(F32)
            for k in xs:
                acc = acc + r_x[k - 1, at].astype(F32)
            s_x[m] = acc.astype(BF16)
            if m:
                cp = remote(s_x.at[m], q_z.at[m - 1], sr.at[26 + m], rr.at[26 + m], **to_z(OFFSET[m]))
                cp.start()
                c2z.append(cp)
        if g == 2:
            for cp in c1z:
                cp.wait()
            acc = hg[a_at(0)].astype(F32)
            for k in zs:
                acc = acc + r_z[k - 1].astype(F32)
            s_z[...] = acc.astype(BF16)
            c2x = []
            for k in xs:
                cp = remote(s_z.at[at_x(k)], q_x.at[k - 1], sr.at[23 + k], rr.at[23 + k], **to_x(k))
                cp.start()
                c2x.append(cp)
        if g == 3:
            for cp in wcp:
                cp.wait()
            w_out[c, mine_x, :] = w_g[...]
            wcp = []
            for k in xs:
                cp = remote(w_g, w_out.at[c, mine_x, :], sw.at[20 + k], rw.at[20 + k], **to_x(k))
                cp.start()
                wcp.append(cp)

        if g == 0:
            for cp in wcp:
                cp.wait()
            w_core = remote(w_out.at[c], w_out.at[c], sw.at[24], rw.at[24], **to_core)
            w_core.start()

    own_d.wait()
    for cp in dcp:
        cp.wait()

    def finish(s, carry):
        at = pl.ds(pl.multiple_of(s * BLK, BLK), BLK)
        gf_ref[:, at] = (dx[:, at].astype(F32) + terms0[plan[3, s]]).astype(BF16)
        return carry

    lax.fori_loop(BND, RB, finish, 0, unroll=10)
    tail = pl.ds(BND * BLK, (RB - BND) * BLK)
    put_tail = pltpu.make_async_copy(gf_ref.at[:, tail], gf_hbm.at[:, tail], loc.at[25])
    put_tail.start()
    w_core.wait()
    puts = []
    for core in range(NC):
        for i, dst in enumerate((gs_hbm, gn_hbm)):
            cp = pltpu.make_async_copy(
                w_out.at[core, pl.ds(i * F, F), :],
                dst.at[:, pl.ds(core * half_h, half_h)],
                loc.at[27 + 2 * core + i],
            )
            cp.start()
            puts.append(cp)
    for cp in c2x + c2z:
        cp.wait()
    for j in range(BND):
        at = pl.ds(j * BLK, BLK)
        acc = dx[:, at].astype(F32) + terms0[plan[3, j]]
        if j < JB:
            acc = acc + s_x[0, j].astype(F32)
            for k in zs:
                acc = acc + q_z[k - 1, j].astype(F32)
        else:
            acc = acc + s_z[x].astype(F32)
            for k in xs:
                acc = acc + q_x[k - 1].astype(F32)
        gf_ref[:, at] = acc.astype(BF16)

    head = pl.ds(0, BND * BLK)
    put_head = pltpu.make_async_copy(gf_ref.at[:, head], gf_hbm.at[:, head], loc.at[26])
    put_head.start()

    for cp in out_copies + puts + [put_tail, put_head]:
        cp.wait()


def emit_kernel(*refs):
    sems = refs[12]
    pieces = []
    for src, dst, held in zip(refs[:4], refs[4:8], refs[8:12]):
        rows = min(src.shape[0], max(16, src.shape[0] // EMIT_PARTS // 16 * 16)) if src.dtype == BF16 else src.shape[0]
        parts = src.shape[0] // rows
        for p in range(parts):
            at = pl.ds(p * rows, rows)
            n = 2 * len(pieces)
            into = pltpu.make_async_copy(src.at[at, :], held.at[at, :], sems.at[n])
            into.start()
            pieces.append((into, pltpu.make_async_copy(held.at[at, :], dst.at[at, :], sems.at[n + 1])))
    for into, out in pieces:
        into.wait()
        out.start()
    for _, out in pieces:
        out.wait()


def shards(node_feats, adj_cols, adj_vals, send_list, send_count, w_self, w_neigh, cotangent):
    cols = adj_cols.T
    lists = send_list.reshape(NX * NZ, NC * N_DOM, CAP).transpose(0, 2, 1)
    counts = send_count.reshape(NX * NZ, NC * N_DOM)
    smem = pl.BlockSpec(memory_space=pltpu.SMEM)
    vmem = pl.BlockSpec(memory_space=pltpu.VMEM)
    hbm = pl.BlockSpec(memory_space=pl.ANY)
    vm = pltpu.VMEM
    dma = pltpu.SemaphoreType.DMA
    half_h = H // NC
    step_x = 2 * F // NX
    step_z = step_x // NZ
    scratch = [
        vm((NX * NZ, CAP, NC * N_DOM), jnp.int32),
        vm((NX * NZ, NC * N_DOM), jnp.int32),
        vm((2 * F, H), BF16),
        vm((FL, RB * BLK), BF16),
        vm((FL, RB * BLK), BF16),
        vm((RB, 2, BLK, BLK), BF16),
        vm((ROWS, H), BF16),
        vm((ROWS, H), BF16),
        vm((HALO + 1, FL, BLK), BF16),
        vm((F, ROWS), BF16),
        vm((F, ROWS), BF16),
        vm((FL, RB * BLK), BF16),
        vm((ROWS, H), BF16),
        vm((F, ROWS), BF16),
        vm((F, ROWS), BF16),
        vm((FL, RB * BLK), BF16),
        vm((FL, RB * BLK), BF16),
        vm((RB, FL, BLK), BF16),
        vm((RB + 1, FL, BLK), F32),
        vm((RB + 1, FL, BLK), F32),
        vm((HALO, FL, BLK), BF16),
        vm((NX * NZ * BND, FL, BLK), BF16),
        vm((NX - 1, NZ * JB, FL, BLK), BF16),
        vm((NZ - 1, NX, FL, BLK), BF16),
        vm((NZ, JB, FL, BLK), BF16),
        vm((NZ - 1, JB, FL, BLK), BF16),
        vm((NX - 1, FL, BLK), BF16),
        vm((NX, FL, BLK), BF16),
        vm((NC, 2 * F, half_h), F32),
        vm((2 * F, half_h), F32),
        vm((2 * F, half_h), F32),
        vm((step_x, half_h), F32),
        vm((NX - 1, step_x, half_h), F32),
        vm((NZ - 1, step_z, half_h), F32),
        vm((NY, step_z, half_h), F32),
        vm((step_x, half_h), F32),
        vm((NC, 2 * F, half_h), F32),
        vm((8, BLK), jnp.int32),
        vm((8, BLK), jnp.int32),
        pltpu.SMEM((8, BLK), jnp.int32),
        dma((35,)),
        dma((3,)),
        dma((3,)),
        dma((9,)),
        dma((9,)),
        dma((9,)),
        dma((9,)),
        dma((3,)),
        dma((3,)),
        dma((42,)),
        dma((42,)),
        dma((34,)),
        dma((34,)),
        dma((25,)),
        dma((25,)),
    ]
    results = pl.pallas_call(
        functools.partial(layer_kernel, 1.0 / math.sqrt(RB * BLK * N_DOM)),
        out_shape=(
            jax.ShapeDtypeStruct((ROWS, H), BF16),
            jax.ShapeDtypeStruct((F, H), F32),
            jax.ShapeDtypeStruct((F, H), F32),
            jax.ShapeDtypeStruct((FL, RB * BLK), BF16),
        ),
        in_specs=[smem, vmem] + [hbm] * 7,
        out_specs=(hbm, hbm, hbm, hbm),
        scratch_shapes=scratch,
        compiler_params=pltpu.CompilerParams(
            collective_id=0, has_side_effects=True, vmem_limit_bytes=56 * 1024 * 1024
        ),
        cost_estimate=pl.CostEstimate(flops=1_800_000_000, bytes_accessed=14_000_000, transcendentals=852_000),
        name="layer",
    )(cols, cols, lists, counts, w_self, w_neigh, node_feats, adj_vals, cotangent)
    return pl.pallas_call(
        emit_kernel,
        out_shape=[jax.ShapeDtypeStruct(a.shape, a.dtype) for a in results],
        in_specs=[hbm] * 4,
        out_specs=[hbm] * 4,
        scratch_shapes=[vm(a.shape, a.dtype) for a in results] + [dma((4 * EMIT_PARTS + 4,))],
        compiler_params=pltpu.CompilerParams(vmem_limit_bytes=56 * 1024 * 1024),
        name="emit",
    )(*results)


def solution(mesh):
    return jax.shard_map(
        shards,
        mesh=mesh,
        in_specs=(
            P("feat", "dom"),
            P("dom", None),
            P("dom", None, None, None),
            P(),
            P(),
            P(),
            P(),
            P(("dom", "feat"), None),
        ),
        out_specs=(P(("dom", "feat"), None), P(), P(), P("feat", "dom")),
        check_vma=False,
    )
```
